32 devices in a mesh: dp: 4 (over y, x), grp: 4 (over z), loc: 2 (over core).
Axes of the slice: x: 2, y: 2, z: 4, core: 2. Of those that a mesh axis runs over, the one named last changes fastest.
Arguments:
- tokens: bfloat16 [1024, 2048], P(('grp', 'loc'), 'dp'), may hold values from -6 to 6
- grad_out: bfloat16 [1024, 2048], P(('grp', 'loc'), 'dp'), may hold values from -6 to 6
- expert_ids: int32 [1024, 4], P(('grp', 'loc')), may hold values from 0 to 7, all different within a row; in each aligned block of 128 rows (0 to 127, 128 to 255, ...) at most 128 rows name the same one
- gate_scale: float32 [1024, 4], P(('grp', 'loc')), may hold values from 0.1 to 1
- gate_weight: bfloat16 [8, 768, 2048], P(('grp', 'loc'), 'dp'), may hold values from -0.125 to 0.125
- up_weight: bfloat16 [8, 768, 2048], P(('grp', 'loc'), 'dp'), may hold values from -0.125 to 0.125
- down_weight: bfloat16 [8, 768, 2048], P(('grp', 'loc'), None, 'dp'), may hold values from -0.21875 to 0.21875
Outputs:
- layer_out: bfloat16 [1024, 2048], P(('grp', 'loc'), 'dp')
- gate_gradient: bfloat16 [8, 768, 2048], P(('grp', 'loc'), 'dp')
- up_gradient: bfloat16 [8, 768, 2048], P(('grp', 'loc'), 'dp')
- down_gradient: bfloat16 [8, 768, 2048], P(('grp', 'loc'), None, 'dp')
The draws below stay inside these ranges and needn't reach their ends.
Inputs may be any that keep to these rules, and one draw needn't show every extreme that they name: `expert_ids`: each token names 4 different experts. Within one index of grp and loc (aligned blocks of 128 token rows) no expert is named by more than 128 rows, a bound that some block reaches.
All inputs are finite; a program needn't handle non-finite values.
Results may differ from the reference program's by a relative error of at most 0.0058.
Values may be sent and summed in bfloat16 or wider, within the bound.
No kernel may reach another device: no remote copies, remote signals or barrier semaphores. Data moves between devices by JAX's collectives and lax.ppermute only.
A program may use at most 64 MiB of HBM per device.

```python
import math
import jax
import jax.numpy as jnp
import numpy as np
from jax import lax

D = 2048
F = 768
TOP = 4
TOK_DEV = 128
EXPERTS = 8
CAP = 128
TOKENS = 1024


def steps_of(rng, shape, cuts, least, largest):
    gain = 1.0
    for position, parts in cuts:
        draws = jax.random.uniform(jax.random.fold_in(jax.random.fold_in(rng, 6), position), (parts,), jnp.float32, least / len(cuts), largest / len(cuts))
        gain = gain * jnp.repeat(jnp.exp(draws), shape[position] // parts).reshape((-1,) + (1,) * (len(shape) - 1 - position))
    return gain


def assign_block(stream_key, own, number, rows, amount, top, limit, skew):
    ranking = jax.random.permutation(stream_key, amount)
    heavy_load, common = load_shares(amount, rows * top, limit, skew, True), load_shares(amount, rows * top, limit, skew, False)
    places = jnp.arange(amount)

    def named(sizes, offset_by):
        used = int((sizes > 0).sum())
        fixed = max(1, used // 4)
        shifted = fixed + (places - fixed + offset_by * (used - fixed)) % max(1, amount - fixed)
        return jnp.zeros((amount,), jnp.int32).at[ranking[jnp.where(places < fixed, places, shifted)]].set(jnp.asarray(sizes, jnp.int32))

    sizes = jnp.where(number % 4 == 0, named(heavy_load, number // 4), named(common, number - number // 4 - 1))
    mixed = jax.random.permutation(jax.random.fold_in(own, 3), amount)
    source_of, sink = mixed[0:amount // 2 * 2:2], mixed[1:amount // 2 * 2:2]
    slack = jnp.minimum(sizes[source_of] - 1, limit - sizes[sink]) // 2
    slack = jnp.where((source_of == ranking[0]) | (sink == ranking[0]) | (sizes[sink] == 0), 0, jnp.maximum(slack, 0))
    shifted = jax.random.randint(jax.random.fold_in(own, 4), (amount // 2,), 0, 1 << 20) % (slack + 1)
    sizes = sizes.at[source_of].add(-shifted).at[sink].add(shifted)
    members = jnp.searchsorted(jnp.cumsum(sizes), jnp.arange(rows * top), side="right").astype(jnp.int32)
    grid = members.reshape(top, rows).T
    grid = grid[jax.random.permutation(jax.random.fold_in(own, 1), rows)]
    offset_by = jax.random.randint(jax.random.fold_in(own, 2), (rows, 1), 0, top)
    return jnp.take_along_axis(grid, (jnp.arange(top)[None, :] + offset_by) % top, axis=1)


def load_shares(number_of, total, bound, slope, full):
    portions = [(1 << 20) // math.isqrt(grade ** slope) + 1 for grade in range(1, number_of + 1)]
    largest = bound if full else min(bound, max(-(-total // number_of), total * portions[0] // sum(portions)))
    least = 1 if total - largest >= number_of - 1 else 0
    holding, surplus = [largest] + [least] * (number_of - 1), total - largest - least * (number_of - 1)
    while surplus > 0:
        movable = [i for i in range(1, number_of) if holding[i] < largest] or [i for i in range(1, number_of) if holding[i] < bound]
        whole, remaining = sum([portions[i] for i in movable]), surplus
        for i in movable:
            addition = min(bound - holding[i], max(1, remaining * portions[i] // whole), surplus)
            holding[i] = holding[i] + addition
            surplus = surplus - addition
    return np.array(holding)


def bell_draw(own_key, shape, width, most, shards=(), held_as=jnp.bfloat16):
    values = jax.random.normal(own_key, shape, jnp.float32) * width
    if len(shards) > 0:
        values = steps_of(own_key, shape, shards, -0.22, 0.18) * values
    return jnp.clip(values, min=-most, max=most).astype(held_as)


def setup_inputs(seed: int = 0) -> dict:
    seeds = jax.random.split(jax.random.key(seed), 8)
    tokens = bell_draw(seeds[0], (TOKENS, D), 1.0, 6.0, ((0, 8), (1, 4)))
    grad_out = bell_draw(seeds[1], (TOKENS, D), 1.0, 6.0, ((0, 8), (1, 4)))
    expert_ids_keys = jax.random.split(jax.random.fold_in(seeds[2], 1), TOKENS // TOK_DEV)
    expert_ids_turns = jax.random.permutation(jax.random.fold_in(seeds[2], 3), TOKENS // TOK_DEV)
    expert_ids = jax.vmap(lambda own, number: assign_block(jax.random.fold_in(seeds[2], 2), own, number, TOK_DEV, EXPERTS, TOP, CAP, 2))(expert_ids_keys, expert_ids_turns).reshape((TOKENS, TOP))
    gate_scale = jnp.clip(jnp.exp(math.log(1.0) - 2.3025851 * jax.random.uniform(seeds[3], (TOKENS, TOP), jnp.float32) ** steps_of(seeds[3], (TOKENS, TOP), ((0, 8),), -0.2, 0.2)), 0.1, 1.0)
    gate_weight = bell_draw(seeds[4], (EXPERTS, F, D), D ** -0.5, 0.125, ((0, 8), (1, 4)))
    up_weight = bell_draw(seeds[5], (EXPERTS, F, D), D ** -0.5, 0.125, ((0, 8), (1, 4)))
    down_weight = bell_draw(seeds[6], (EXPERTS, F, D), F ** -0.5, 0.21875, ((0, 8), (2, 4)))
    return {"tokens": tokens, "grad_out": grad_out, "expert_ids": expert_ids, "gate_scale": gate_scale, "gate_weight": gate_weight, "up_weight": up_weight, "down_weight": down_weight}


def reference(tokens, grad_out, expert_ids, gate_scale, gate_weight, up_weight, down_weight):
    columns = TOKENS // TOK_DEV
    per_column = TOK_DEV * TOP
    column_ids = expert_ids.reshape(columns, per_column).astype(jnp.int32)
    onehot = (column_ids[:, :, None] == jnp.arange(EXPERTS, dtype=jnp.int32)[None, None, :]).astype(jnp.int32)
    ranks = jnp.sum((jnp.cumsum(onehot, axis=1) - 1) * onehot, axis=2).astype(jnp.int32)
    column_index = jnp.arange(columns, dtype=jnp.int32)[:, None]
    buffer_row = column_index * CAP + ranks
    token_index = column_index * TOK_DEV + jnp.arange(per_column, dtype=jnp.int32)[None, :] // TOP
    rows_total = columns * CAP
    flat_ids = column_ids.reshape(-1)
    flat_rows = buffer_row.reshape(-1)
    token_table = jnp.full((EXPERTS, rows_total), TOKENS, jnp.int32).at[flat_ids, flat_rows].set(token_index.reshape(-1).astype(jnp.int32))
    scale_table = jnp.zeros((EXPERTS, rows_total), jnp.float32).at[flat_ids, flat_rows].set(gate_scale.reshape(-1).astype(jnp.float32))
    padded_tokens = jnp.concatenate([tokens, jnp.zeros((1, D), tokens.dtype)], axis=0)
    padded_grad = jnp.concatenate([grad_out, jnp.zeros((1, D), grad_out.dtype)], axis=0)

    def one_expert(total, inputs):
        table_row, scale_row, gate_mat, up_mat, down_mat = inputs
        slot_tokens = padded_tokens[table_row]
        gate_pre = jnp.dot(slot_tokens, gate_mat.T, preferred_element_type=jnp.float32)
        up_pre = jnp.dot(slot_tokens, up_mat.T, preferred_element_type=jnp.float32)
        sigmoid_gate = jax.nn.sigmoid(gate_pre)
        activated = gate_pre * sigmoid_gate
        hidden = (activated * up_pre).astype(jnp.bfloat16)
        expert_out = jnp.dot(hidden, down_mat, preferred_element_type=jnp.float32).astype(jnp.bfloat16)
        total = total.at[table_row].add(scale_row[:, None] * expert_out.astype(jnp.float32))
        slot_grad = (scale_row[:, None] * padded_grad[table_row].astype(jnp.float32)).astype(jnp.bfloat16)
        hidden_grad = jnp.dot(slot_grad, down_mat.T, preferred_element_type=jnp.float32)
        gate_grad = (hidden_grad * up_pre * sigmoid_gate * (1.0 + gate_pre * (1.0 - sigmoid_gate))).astype(jnp.bfloat16)
        up_grad = (hidden_grad * activated).astype(jnp.bfloat16)
        down_out = jnp.dot(hidden.T, slot_grad, preferred_element_type=jnp.float32).astype(jnp.bfloat16)
        gate_out = jnp.dot(gate_grad.T, slot_tokens, preferred_element_type=jnp.float32).astype(jnp.bfloat16)
        up_out = jnp.dot(up_grad.T, slot_tokens, preferred_element_type=jnp.float32).astype(jnp.bfloat16)
        return total, (gate_out, up_out, down_out)

    start = jnp.zeros((TOKENS + 1, D), jnp.float32)
    total, grads = lax.scan(one_expert, start, (token_table, scale_table, gate_weight, up_weight, down_weight))
    return total[:TOKENS].astype(jnp.bfloat16), grads[0], grads[1], grads[2]
```

```python
import jax
import jax.numpy as jnp
from jax import lax
from jax.sharding import PartitionSpec as P


def slot_layout(route_ids, experts, capacity):
    flat_ids = route_ids.reshape(-1)
    onehot = (
        flat_ids[:, None] == lax.broadcasted_iota(jnp.int32, (flat_ids.shape[0], experts), 1)
    ).astype(jnp.int32)
    ranks = jnp.sum((jnp.cumsum(onehot, axis=0) - 1) * onehot, axis=1)
    return flat_ids * capacity + ranks


def place_matrix(positions, tok_rows, per_token, slots_total):
    slot_index = lax.broadcasted_iota(jnp.int32, (slots_total, tok_rows, per_token), 0)
    hits = slot_index == positions.reshape(1, tok_rows, per_token)
    return jnp.sum(hits.astype(jnp.float32), axis=2).astype(jnp.bfloat16)


def send_rows(outgoing):
    return lax.all_to_all(outgoing, ("grp", "loc"), split_axis=0, concat_axis=0, tiled=True)


def return_rows(results):
    return lax.all_to_all(results, ("grp", "loc"), split_axis=0, concat_axis=0, tiled=True)


def slot_body(tokens, grad_out, expert_ids, gate_scale, gate_weight, up_weight, down_weight):
    tok_rows, quarter = tokens.shape
    per_token = expert_ids.shape[1]
    experts = lax.axis_size(("grp", "loc"))
    capacity = min(tok_rows, max(2, 2 * tok_rows * per_token // experts))
    slots_total = experts * capacity
    positions = slot_layout(expert_ids, experts, capacity)
    unit_place = place_matrix(positions, tok_rows, per_token, slots_total)
    slot_scale = jnp.zeros((slots_total,), jnp.float32).at[positions].set(gate_scale.reshape(-1))
    picked_grads = jnp.dot(unit_place, grad_out, preferred_element_type=jnp.float32)
    grad_rows = (picked_grads * slot_scale[:, None]).astype(jnp.bfloat16)
    full_tokens = lax.all_gather(tokens, "dp", axis=1, tiled=True)
    features = full_tokens.shape[1]
    token_rows = jnp.dot(unit_place, full_tokens, preferred_element_type=jnp.float32).astype(
        jnp.bfloat16
    )
    outgoing = jnp.concatenate([token_rows, grad_rows], axis=1).reshape(
        experts, capacity, features + quarter
    )
    arrived = send_rows(outgoing)
    slot_tokens = arrived[:, :, :features]
    slot_grads = arrived[:, :, features:]
    flat_tokens = slot_tokens.reshape(slots_total, -1)
    flat_grads = slot_grads.reshape(slots_total, quarter)
    gate_mat = gate_weight[0]
    up_mat = up_weight[0]
    down_mat = down_weight[0]
    feature_contract = (((1,), (1,)), ((), ()))
    gate_pre = lax.dot_general(
        gate_mat, flat_tokens, feature_contract, preferred_element_type=jnp.float32
    )
    up_pre = lax.dot_general(
        up_mat, flat_tokens, feature_contract, preferred_element_type=jnp.float32
    )
    sigmoid_gate = jax.nn.sigmoid(gate_pre)
    activated = gate_pre * sigmoid_gate
    hidden = (activated * up_pre).astype(jnp.bfloat16)
    piece = lax.all_gather(hidden, "dp", axis=0, tiled=True)
    down_rows = down_mat
    out_total = lax.dot_general(
        piece, down_rows, (((0,), (0,)), ((), ())), preferred_element_type=jnp.float32
    )
    block_grad = jnp.dot(piece, flat_grads, preferred_element_type=jnp.float32)
    down_total = block_grad
    out_total, down_total = (out_total, down_total)
    expert_out = out_total.astype(jnp.bfloat16)
    down_gradient = down_total.astype(jnp.bfloat16)
    returned = return_rows(expert_out.reshape(experts, capacity, quarter)).reshape(
        slots_total, quarter
    )
    picked = returned[positions].astype(jnp.float32) * gate_scale.reshape(-1)[:, None]
    layer_out = jnp.sum(picked.reshape(tok_rows, per_token, quarter), axis=1).astype(jnp.bfloat16)
    down_rows = down_mat
    hidden_grad = lax.psum_scatter(
        lax.dot_general(
            down_rows, flat_grads, feature_contract, preferred_element_type=jnp.float32
        ),
        "dp",
        scatter_dimension=0,
        tiled=True,
    )
    gate_grad = (
        hidden_grad * up_pre * sigmoid_gate * (1.0 + gate_pre * (1.0 - sigmoid_gate))
    ).astype(jnp.bfloat16)
    up_grad = (hidden_grad * activated).astype(jnp.bfloat16)
    gate_gradient = jnp.dot(gate_grad, flat_tokens, preferred_element_type=jnp.float32).astype(
        jnp.bfloat16
    )
    up_gradient = jnp.dot(up_grad, flat_tokens, preferred_element_type=jnp.float32).astype(
        jnp.bfloat16
    )
    return (layer_out, gate_gradient[None], up_gradient[None], down_gradient[None])


GROUPS = ((0, 1), (2, 3))


def swap(value, axis, bit):
    pairs = [(i, i ^ bit) for i in range(lax.axis_size(axis))]
    return lax.ppermute(value, axis, pairs)


def square_gather(own):
    near_x, near_y = swap(own, "dp", 1), swap(own, "dp", 2)
    half = own.shape[0] // 2
    far = jnp.concatenate([swap(near_x[:half], "dp", 2), swap(near_y[half:], "dp", 1)], axis=0)
    return [own, near_x, near_y, far]


def square_scatter(parts):
    far = parts[3].astype(jnp.bfloat16)
    half = far.shape[0] // 2
    top, bottom = swap(far[:half], "dp", 2), swap(far[half:], "dp", 1)
    for_x = jnp.concatenate([parts[1][:half] + top.astype(jnp.float32), parts[1][half:]], axis=0)
    for_y = jnp.concatenate([parts[2][:half], parts[2][half:] + bottom.astype(jnp.float32)], axis=0)
    from_x = swap(for_x.astype(jnp.bfloat16), "dp", 1)
    from_y = swap(for_y.astype(jnp.bfloat16), "dp", 2)
    return parts[0] + from_x.astype(jnp.float32) + from_y.astype(jnp.float32)


def regroup(value, axis, place):
    size = value.shape[axis] // 4
    return jnp.concatenate(
        [lax.dynamic_slice_in_dim(value, (place ^ j) * size, size, axis) for j in range(4)], axis=axis
    )


def dense_body(tokens, grad_out, expert_ids, gate_scale, gate_weight, up_weight, down_weight):
    rows, quarter = tokens.shape
    experts = lax.axis_size(("grp", "loc"))
    place = lax.axis_index("dp")
    expert = lax.axis_index(("grp", "loc"))
    units = gate_weight.shape[1]
    contract_last = (((1,), (1,)), ((), ()))
    contract_first = (((0,), (0,)), ((), ()))

    named = lax.broadcasted_iota(jnp.int32, (experts, rows, 1), 0) == expert_ids[None]
    scales = jnp.sum(jnp.where(named, gate_scale[None], 0.0), axis=2)
    span = range(lax.axis_size("grp"))
    token_blocks = [tokens if j == 0 else swap(tokens, "grp", j) for j in span]
    grad_blocks = [grad_out if j == 0 else swap(grad_out, "grp", j) for j in span]
    scale_blocks = jnp.stack([scales if j == 0 else swap(scales, "grp", j) for j in span])
    scale_other = swap(scale_blocks, "loc", 1)
    scale_own = lax.dynamic_index_in_dim(scale_blocks, expert, 1, keepdims=False)
    scale_other = lax.dynamic_index_in_dim(scale_other, expert, 1, keepdims=False)

    in_weights = regroup(jnp.concatenate([gate_weight[0], up_weight[0]], axis=0), 1, place)
    down_rows = regroup(down_weight[0], 0, place)

    all_tokens, all_hidden, gate_factors, up_factors, grads, pieces = [], [], [], [], [], []
    for group in GROUPS:
        own = square_gather(jnp.concatenate([token_blocks[j] for j in group], axis=0))
        own = jnp.concatenate(own, axis=1)
        both = jnp.concatenate([own, swap(own, "loc", 1)], axis=0)
        all_tokens.append(both)
        pre = lax.dot_general(in_weights, both, contract_last, preferred_element_type=jnp.float32)
        scale = jnp.concatenate([s[j] for s in (scale_own, scale_other) for j in group])[None]
        gate_pre, up_pre = pre[:units], pre[units:]
        sig = jax.nn.sigmoid(gate_pre)
        activated = gate_pre * sig
        hidden = (activated * up_pre * scale).astype(jnp.bfloat16)
        gate_factors.append(up_pre * sig * (1.0 + gate_pre * (1.0 - sig)) * scale)
        up_factors.append(activated * scale)
        hidden = jnp.concatenate(square_gather(hidden), axis=0)
        all_hidden.append(hidden)
        out = lax.dot_general(hidden, down_rows, contract_first, preferred_element_type=jnp.float32)
        half = out.shape[0] // 2
        mine = out[:half] + swap(out[half:].astype(jnp.bfloat16), "loc", 1).astype(jnp.float32)
        for i, j in enumerate(group):
            block = mine[i * rows : (i + 1) * rows]
            pieces.append(block if j == 0 else swap(block.astype(jnp.bfloat16), "grp", j).astype(jnp.float32))
        grads_own = jnp.concatenate([grad_blocks[j] for j in group], axis=0)
        grads.append(jnp.concatenate([grads_own, swap(grads_own, "loc", 1)], axis=0))
    layer_out = sum(pieces).astype(jnp.bfloat16)
    grads = jnp.concatenate(grads, axis=0)
    all_tokens = jnp.concatenate(all_tokens, axis=0)
    all_hidden = jnp.concatenate(all_hidden, axis=1)
    shares = lax.dot_general(down_rows, grads, contract_last, preferred_element_type=jnp.float32)
    hidden_grad = square_scatter([shares[j * units : (j + 1) * units] for j in range(4)])
    down_gradient = jnp.dot(all_hidden, grads, preferred_element_type=jnp.float32).astype(jnp.bfloat16)
    both_grads = jnp.concatenate(
        [
            (hidden_grad * jnp.concatenate(gate_factors, axis=1)).astype(jnp.bfloat16),
            (hidden_grad * jnp.concatenate(up_factors, axis=1)).astype(jnp.bfloat16),
        ],
        axis=0,
    )
    in_gradient = jnp.dot(both_grads, all_tokens, preferred_element_type=jnp.float32).astype(jnp.bfloat16)
    in_gradient = regroup(in_gradient, 1, place)
    return (layer_out, in_gradient[None, :units], in_gradient[None, units:], regroup(down_gradient, 0, place)[None])


def body(tokens, grad_out, expert_ids, *rest):
    experts = lax.axis_size(("grp", "loc"))
    rows, per_token = expert_ids.shape
    square = lax.axis_size("dp") == 4 and lax.axis_size("grp") == 4 and lax.axis_size("loc") == 2
    if square and 2 * rows * per_token // experts >= rows:
        return dense_body(tokens, grad_out, expert_ids, *rest)
    return slot_body(tokens, grad_out, expert_ids, *rest)


def solution(mesh):
    return jax.shard_map(
        body,
        mesh=mesh,
        in_specs=(
            P(("grp", "loc"), "dp"),
            P(("grp", "loc"), "dp"),
            P(("grp", "loc"), None),
            P(("grp", "loc"), None),
            P(("grp", "loc"), "dp", None),
            P(("grp", "loc"), "dp", None),
            P(("grp", "loc"), None, "dp"),
        ),
        out_specs=(
            P(("grp", "loc"), "dp"),
            P(("grp", "loc"), "dp", None),
            P(("grp", "loc"), "dp", None),
            P(("grp", "loc"), None, "dp"),
        ),
        check_vma=False,
    )
```

```python
import jax
import jax.numpy as jnp
from jax import lax
from jax.sharding import PartitionSpec as P


def slot_layout(route_ids, experts, capacity):
    flat_ids = route_ids.reshape(-1)
    onehot = (
        flat_ids[:, None] == lax.broadcasted_iota(jnp.int32, (flat_ids.shape[0], experts), 1)
    ).astype(jnp.int32)
    ranks = jnp.sum((jnp.cumsum(onehot, axis=0) - 1) * onehot, axis=1)
    return flat_ids * capacity + ranks


def place_matrix(positions, tok_rows, per_token, slots_total):
    slot_index = lax.broadcasted_iota(jnp.int32, (slots_total, tok_rows, per_token), 0)
    hits = slot_index == positions.reshape(1, tok_rows, per_token)
    return jnp.sum(hits.astype(jnp.float32), axis=2).astype(jnp.bfloat16)


def send_rows(outgoing):
    return lax.all_to_all(outgoing, ("grp", "loc"), split_axis=0, concat_axis=0, tiled=True)


def return_rows(results):
    return lax.all_to_all(results, ("grp", "loc"), split_axis=0, concat_axis=0, tiled=True)


def slot_body(tokens, grad_out, expert_ids, gate_scale, gate_weight, up_weight, down_weight):
    tok_rows, quarter = tokens.shape
    per_token = expert_ids.shape[1]
    experts = lax.axis_size(("grp", "loc"))
    capacity = min(tok_rows, max(2, 2 * tok_rows * per_token // experts))
    slots_total = experts * capacity
    positions = slot_layout(expert_ids, experts, capacity)
    unit_place = place_matrix(positions, tok_rows, per_token, slots_total)
    slot_scale = jnp.zeros((slots_total,), jnp.float32).at[positions].set(gate_scale.reshape(-1))
    picked_grads = jnp.dot(unit_place, grad_out, preferred_element_type=jnp.float32)
    grad_rows = (picked_grads * slot_scale[:, None]).astype(jnp.bfloat16)
    full_tokens = lax.all_gather(tokens, "dp", axis=1, tiled=True)
    features = full_tokens.shape[1]
    token_rows = jnp.dot(unit_place, full_tokens, preferred_element_type=jnp.float32).astype(
        jnp.bfloat16
    )
    outgoing = jnp.concatenate([token_rows, grad_rows], axis=1).reshape(
        experts, capacity, features + quarter
    )
    arrived = send_rows(outgoing)
    slot_tokens = arrived[:, :, :features]
    slot_grads = arrived[:, :, features:]
    flat_tokens = slot_tokens.reshape(slots_total, -1)
    flat_grads = slot_grads.reshape(slots_total, quarter)
    gate_mat = gate_weight[0]
    up_mat = up_weight[0]
    down_mat = down_weight[0]
    feature_contract = (((1,), (1,)), ((), ()))
    gate_pre = lax.dot_general(
        gate_mat, flat_tokens, feature_contract, preferred_element_type=jnp.float32
    )
    up_pre = lax.dot_general(
        up_mat, flat_tokens, feature_contract, preferred_element_type=jnp.float32
    )
    sigmoid_gate = jax.nn.sigmoid(gate_pre)
    activated = gate_pre * sigmoid_gate
    hidden = (activated * up_pre).astype(jnp.bfloat16)
    piece = lax.all_gather(hidden, "dp", axis=0, tiled=True)
    down_rows = down_mat
    out_total = lax.dot_general(
        piece, down_rows, (((0,), (0,)), ((), ())), preferred_element_type=jnp.float32
    )
    block_grad = jnp.dot(piece, flat_grads, preferred_element_type=jnp.float32)
    down_total = block_grad
    out_total, down_total = (out_total, down_total)
    expert_out = out_total.astype(jnp.bfloat16)
    down_gradient = down_total.astype(jnp.bfloat16)
    returned = return_rows(expert_out.reshape(experts, capacity, quarter)).reshape(
        slots_total, quarter
    )
    picked = returned[positions].astype(jnp.float32) * gate_scale.reshape(-1)[:, None]
    layer_out = jnp.sum(picked.reshape(tok_rows, per_token, quarter), axis=1).astype(jnp.bfloat16)
    down_rows = down_mat
    hidden_grad = lax.psum_scatter(
        lax.dot_general(
            down_rows, flat_grads, feature_contract, preferred_element_type=jnp.float32
        ),
        "dp",
        scatter_dimension=0,
        tiled=True,
    )
    gate_grad = (
        hidden_grad * up_pre * sigmoid_gate * (1.0 + gate_pre * (1.0 - sigmoid_gate))
    ).astype(jnp.bfloat16)
    up_grad = (hidden_grad * activated).astype(jnp.bfloat16)
    gate_gradient = jnp.dot(gate_grad, flat_tokens, preferred_element_type=jnp.float32).astype(
        jnp.bfloat16
    )
    up_gradient = jnp.dot(up_grad, flat_tokens, preferred_element_type=jnp.float32).astype(
        jnp.bfloat16
    )
    return (layer_out, gate_gradient[None], up_gradient[None], down_gradient[None])


def swap(value, axis, bit):
    pairs = [(i, i ^ bit) for i in range(lax.axis_size(axis))]
    return lax.ppermute(value, axis, pairs)


def spread(value):
    return [swap(value, "dp", j) for j in (1, 2, 3)]


def to_core(value):
    return swap(value, "loc", 1)


def stack(*values):
    return jnp.concatenate(values, axis=0)


def beside(*values):
    return jnp.concatenate(values, axis=1)


def phase(*values):
    return lax.optimization_barrier(values)


def regroup(value, axis, place):
    size = value.shape[axis] // 4
    return jnp.concatenate(
        [lax.dynamic_slice_in_dim(value, (place ^ j) * size, size, axis) for j in range(4)], axis=axis
    )


def activate(pre):
    units = pre.shape[0] // 2
    gate_pre, up_pre = pre[:units], pre[units:]
    sig = jax.nn.sigmoid(gate_pre)
    activated = gate_pre * sig
    return (activated * up_pre).astype(jnp.bfloat16), up_pre * sig * (1.0 + gate_pre * (1.0 - sig)), activated


def dense_body(tokens, grad_out, expert_ids, gate_scale, gate_weight, up_weight, down_weight):
    rows, quarter = tokens.shape
    experts = lax.axis_size(("grp", "loc"))
    place = lax.axis_index("dp")
    expert = lax.axis_index(("grp", "loc"))
    units = gate_weight.shape[1]
    half = units // 2
    contract_last = (((1,), (1,)), ((), ()))
    contract_first = (((0,), (0,)), ((), ()))
    wide = dict(preferred_element_type=jnp.float32)
    half_type, wide_type = jnp.bfloat16, jnp.float32

    t2, t3 = swap(tokens, "grp", 2), swap(tokens, "grp", 3)
    p0 = [tokens] + spread(tokens)
    in_weights = stack(gate_weight[0], up_weight[0])
    named = lax.broadcasted_iota(jnp.int32, (experts, rows, 1), 0) == expert_ids[None]
    scales = jnp.sum(jnp.where(named, gate_scale[None], 0.0), axis=2)
    high = lax.reduce_precision(scales, 8, 7)
    table = stack(high, scales - high).astype(half_type)
    table = jnp.pad(table, ((0, 0), (0, quarter - rows)))
    payload = stack(grad_out, table)
    far, payload, in_weights, *p0 = phase(stack(t2, t3), payload, in_weights, *p0)

    p2 = [far] + spread(far)
    p1 = swap(stack(*p0), "grp", 1)
    p1, payload, *p2 = phase(p1, payload, *p2)

    g2 = swap(payload, "grp", 2)
    parts = [stack(p0[j], p1[j * rows : (j + 1) * rows], p2[j]) for j in range(4)]
    parts_there = [to_core(p) for p in parts]
    acts = []
    for side in (parts, parts_there):
        pre = 0.0
        for j, part in enumerate(side):
            w_part = lax.dynamic_slice_in_dim(in_weights, (place ^ j) * quarter, quarter, 1)
            pre = pre + lax.dot_general(w_part, part, contract_last, **wide)
        acts.append(activate(pre))
    values = phase(beside(*(a[0] for a in acts)), payload, down_weight, *parts, *parts_there)
    hidden, payload, down_weight, parts, parts_there = values[0], values[1], values[2], values[3:7], values[7:]

    hx, hy = swap(hidden, "dp", 1), swap(hidden, "dp", 2)
    last_x, last_y = swap(hy[half:], "dp", 1), swap(hx[:half], "dp", 2)
    down_rows, payload = phase(regroup(down_weight[0], 0, place), payload)
    g1, g3 = swap(payload, "grp", 1), swap(payload, "grp", 3)
    blocks = jnp.stack([payload, g1, g2, g3])
    blocks = stack(blocks, to_core(blocks))
    table = blocks[:, rows:, :rows].astype(wide_type).reshape(8, 2, experts, rows)
    scale = lax.dynamic_index_in_dim(table, expert, 2, keepdims=False)
    scale = jnp.sum(scale, axis=1).reshape(8 * rows, 1)
    grads = blocks[:, :rows].reshape(8 * rows, quarter).astype(wide_type)
    grads = (grads * scale).astype(half_type)
    shares = lax.dot_general(down_rows, grads, contract_last, **wide).reshape(4, units, -1)
    sent = shares[3].astype(half_type)
    top, bottom = swap(sent[:half], "dp", 2), swap(sent[half:], "dp", 1)
    sums = [
        stack(shares[1][:half] + top.astype(wide_type), shares[1][half:]).astype(half_type),
        stack(shares[2][:half], shares[2][half:] + bottom.astype(wide_type)).astype(half_type),
    ]
    sums = [swap(value, "dp", j + 1) for j, value in enumerate(sums)]
    own_share, *hidden = phase(shares[0], hidden, hx, hy, last_y, last_x)
    hidden = stack(*hidden)

    out = lax.dot_general(hidden, down_rows, contract_first, **wide).astype(half_type).astype(wide_type) * scale
    out = out[: 4 * rows] + to_core(out[4 * rows :].astype(half_type)).astype(wide_type)
    back = out[rows:].astype(half_type)
    back = [swap(back[k * rows : (k + 1) * rows], "grp", k + 1) for k in (1, 0, 2)]
    total, *sums = phase(out[:rows], *sums)
    layer_out = total + back[0].astype(wide_type) + back[1].astype(wide_type) + back[2].astype(wide_type)
    down_gradient = jnp.dot(hidden, grads, **wide)
    down_gradient = regroup(down_gradient.astype(half_type), 0, place)

    hidden_grad = own_share + sums[0].astype(wide_type) + sums[1].astype(wide_type)
    both = []
    for k in range(2):
        side_grad = hidden_grad[:, 4 * k * rows : 4 * (k + 1) * rows]
        both.append(stack(*((side_grad * factor).astype(half_type) for factor in acts[k][1:])))
    in_gradient = [
        jnp.dot(both[0], mine, **wide) + jnp.dot(both[1], other, **wide) for mine, other in zip(parts, parts_there)
    ]
    in_gradient = regroup(beside(*in_gradient).astype(half_type), 1, place)
    return (layer_out.astype(half_type), in_gradient[None, :units], in_gradient[None, units:], down_gradient[None])


def body(tokens, grad_out, expert_ids, *rest):
    experts = lax.axis_size(("grp", "loc"))
    rows, per_token = expert_ids.shape
    square = lax.axis_size("dp") == 4 and lax.axis_size("grp") == 4 and lax.axis_size("loc") == 2
    if square and 2 * rows * per_token // experts >= rows:
        return dense_body(tokens, grad_out, expert_ids, *rest)
    return slot_body(tokens, grad_out, expert_ids, *rest)


def solution(mesh):
    return jax.shard_map(
        body,
        mesh=mesh,
        in_specs=(
            P(("grp", "loc"), "dp"),
            P(("grp", "loc"), "dp"),
            P(("grp", "loc"), None),
            P(("grp", "loc"), None),
            P(("grp", "loc"), "dp", None),
            P(("grp", "loc"), "dp", None),
            P(("grp", "loc"), None, "dp"),
        ),
        out_specs=(
            P(("grp", "loc"), "dp"),
            P(("grp", "loc"), "dp", None),
            P(("grp", "loc"), "dp", None),
            P(("grp", "loc"), None, "dp"),
        ),
        check_vma=False,
    )
```

```python
import jax
import jax.numpy as jnp
from jax import lax
from jax.experimental import pallas as pl
from jax.experimental.pallas import tpu as pltpu
from jax.sharding import PartitionSpec as P


def slot_layout(route_ids, experts, capacity):
    flat_ids = route_ids.reshape(-1)
    onehot = (
        flat_ids[:, None] == lax.broadcasted_iota(jnp.int32, (flat_ids.shape[0], experts), 1)
    ).astype(jnp.int32)
    ranks = jnp.sum((jnp.cumsum(onehot, axis=0) - 1) * onehot, axis=1)
    return flat_ids * capacity + ranks


def place_matrix(positions, tok_rows, per_token, slots_total):
    slot_index = lax.broadcasted_iota(jnp.int32, (slots_total, tok_rows, per_token), 0)
    hits = slot_index == positions.reshape(1, tok_rows, per_token)
    return jnp.sum(hits.astype(jnp.float32), axis=2).astype(jnp.bfloat16)


def send_rows(outgoing):
    return lax.all_to_all(outgoing, ("grp", "loc"), split_axis=0, concat_axis=0, tiled=True)


def return_rows(results):
    return lax.all_to_all(results, ("grp", "loc"), split_axis=0, concat_axis=0, tiled=True)


def slot_body(tokens, grad_out, expert_ids, gate_scale, gate_weight, up_weight, down_weight):
    tok_rows, quarter = tokens.shape
    per_token = expert_ids.shape[1]
    experts = lax.axis_size(("grp", "loc"))
    capacity = min(tok_rows, max(2, 2 * tok_rows * per_token // experts))
    slots_total = experts * capacity
    positions = slot_layout(expert_ids, experts, capacity)
    unit_place = place_matrix(positions, tok_rows, per_token, slots_total)
    slot_scale = jnp.zeros((slots_total,), jnp.float32).at[positions].set(gate_scale.reshape(-1))
    picked_grads = jnp.dot(unit_place, grad_out, preferred_element_type=jnp.float32)
    grad_rows = (picked_grads * slot_scale[:, None]).astype(jnp.bfloat16)
    full_tokens = lax.all_gather(tokens, "dp", axis=1, tiled=True)
    features = full_tokens.shape[1]
    token_rows = jnp.dot(unit_place, full_tokens, preferred_element_type=jnp.float32).astype(
        jnp.bfloat16
    )
    outgoing = jnp.concatenate([token_rows, grad_rows], axis=1).reshape(
        experts, capacity, features + quarter
    )
    arrived = send_rows(outgoing)
    slot_tokens = arrived[:, :, :features]
    slot_grads = arrived[:, :, features:]
    flat_tokens = slot_tokens.reshape(slots_total, -1)
    flat_grads = slot_grads.reshape(slots_total, quarter)
    gate_mat = gate_weight[0]
    up_mat = up_weight[0]
    down_mat = down_weight[0]
    feature_contract = (((1,), (1,)), ((), ()))
    gate_pre = lax.dot_general(
        gate_mat, flat_tokens, feature_contract, preferred_element_type=jnp.float32
    )
    up_pre = lax.dot_general(
        up_mat, flat_tokens, feature_contract, preferred_element_type=jnp.float32
    )
    sigmoid_gate = jax.nn.sigmoid(gate_pre)
    activated = gate_pre * sigmoid_gate
    hidden = (activated * up_pre).astype(jnp.bfloat16)
    piece = lax.all_gather(hidden, "dp", axis=0, tiled=True)
    down_rows = down_mat
    out_total = lax.dot_general(
        piece, down_rows, (((0,), (0,)), ((), ())), preferred_element_type=jnp.float32
    )
    block_grad = jnp.dot(piece, flat_grads, preferred_element_type=jnp.float32)
    down_total = block_grad
    out_total, down_total = (out_total, down_total)
    expert_out = out_total.astype(jnp.bfloat16)
    down_gradient = down_total.astype(jnp.bfloat16)
    returned = return_rows(expert_out.reshape(experts, capacity, quarter)).reshape(
        slots_total, quarter
    )
    picked = returned[positions].astype(jnp.float32) * gate_scale.reshape(-1)[:, None]
    layer_out = jnp.sum(picked.reshape(tok_rows, per_token, quarter), axis=1).astype(jnp.bfloat16)
    down_rows = down_mat
    hidden_grad = lax.psum_scatter(
        lax.dot_general(
            down_rows, flat_grads, feature_contract, preferred_element_type=jnp.float32
        ),
        "dp",
        scatter_dimension=0,
        tiled=True,
    )
    gate_grad = (
        hidden_grad * up_pre * sigmoid_gate * (1.0 + gate_pre * (1.0 - sigmoid_gate))
    ).astype(jnp.bfloat16)
    up_grad = (hidden_grad * activated).astype(jnp.bfloat16)
    gate_gradient = jnp.dot(gate_grad, flat_tokens, preferred_element_type=jnp.float32).astype(
        jnp.bfloat16
    )
    up_gradient = jnp.dot(up_grad, flat_tokens, preferred_element_type=jnp.float32).astype(
        jnp.bfloat16
    )
    return (layer_out, gate_gradient[None], up_gradient[None], down_gradient[None])


def swap(value, axis, bit):
    pairs = [(i, i ^ bit) for i in range(lax.axis_size(axis))]
    return lax.ppermute(value, axis, pairs)


def spread(value):
    return [swap(value, "dp", j) for j in (1, 2, 3)]


def to_core(value):
    return swap(value, "loc", 1)


def stack(*values):
    return jnp.concatenate(values, axis=0)


def beside(*values):
    return jnp.concatenate(values, axis=1)


def phase(*values):
    return lax.optimization_barrier(values)


def regroup(value, axis, place):
    size = value.shape[axis] // 4
    return jnp.concatenate(
        [lax.dynamic_slice_in_dim(value, (place ^ j) * size, size, axis) for j in range(4)], axis=axis
    )


def activate(pre):
    units = pre.shape[0] // 2
    gate_pre, up_pre = pre[:units], pre[units:]
    sig = jax.nn.sigmoid(gate_pre)
    activated = gate_pre * sig
    return (activated * up_pre).astype(jnp.bfloat16), up_pre * sig * (1.0 + gate_pre * (1.0 - sig)), activated


def in_gradients(place, own_share, sums, factors, parts, parts_there):
    units, width = factors[0].shape
    quarter = parts[0].shape[1]

    def kernel(place_ref, share_ref, x_ref, y_ref, *refs):
        factor_refs, part_refs, (gate_ref, up_ref) = refs[:4], refs[4:12], refs[12:]
        total = share_ref[...] + x_ref[...].astype(jnp.float32) + y_ref[...].astype(jnp.float32)
        sides = []
        for k in range(2):
            side = total[:, k * width : (k + 1) * width]
            sides.append([(side * factor_refs[2 * k + i][...]).astype(jnp.bfloat16) for i in range(2)])
        for j in range(4):
            columns = pl.ds(pl.multiple_of((place_ref[0] ^ j) * quarter, quarter), quarter)
            for i, out_ref in enumerate((gate_ref, up_ref)):
                value = jnp.dot(sides[0][i], part_refs[j][...], preferred_element_type=jnp.float32)
                value += jnp.dot(sides[1][i], part_refs[4 + j][...], preferred_element_type=jnp.float32)
                out_ref[:, columns] = value.astype(jnp.bfloat16)

    vmem = pl.BlockSpec(memory_space=pltpu.VMEM)
    return pl.pallas_call(
        kernel,
        out_shape=[jax.ShapeDtypeStruct((units, 4 * quarter), jnp.bfloat16)] * 2,
        in_specs=[pl.BlockSpec(memory_space=pltpu.SMEM)] + [vmem] * 15,
        out_specs=[vmem] * 2,
        compiler_params=pltpu.CompilerParams(vmem_limit_bytes=20 * 2**20),
    )(place, own_share, *sums, *factors, *parts, *parts_there)


def dense_body(tokens, grad_out, expert_ids, gate_scale, gate_weight, up_weight, down_weight):
    rows, quarter = tokens.shape
    experts = lax.axis_size(("grp", "loc"))
    place = lax.axis_index("dp")
    expert = lax.axis_index(("grp", "loc"))
    units = gate_weight.shape[1]
    half = units // 2
    contract_last = (((1,), (1,)), ((), ()))
    contract_first = (((0,), (0,)), ((), ()))
    wide = dict(preferred_element_type=jnp.float32)
    half_type, wide_type = jnp.bfloat16, jnp.float32

    t2, t3 = swap(tokens, "grp", 2), swap(tokens, "grp", 3)
    p0 = [tokens] + spread(tokens)
    in_weights = stack(gate_weight[0], up_weight[0])
    named = lax.broadcasted_iota(jnp.int32, (experts, rows, 1), 0) == expert_ids[None]
    scales = jnp.sum(jnp.where(named, gate_scale[None], 0.0), axis=2)
    high = lax.reduce_precision(scales, 8, 7)
    table = stack(high, scales - high).astype(half_type)
    table = jnp.pad(table, ((0, 0), (0, quarter - rows)))
    payload = stack(grad_out, table)
    own, far, payload, in_weights, *p0 = phase(stack(*p0), stack(t2, t3), payload, in_weights, *p0)

    p1 = swap(own, "grp", 1)
    p2 = [far] + spread(far)
    *p2, payload, p1 = phase(*p2, payload, p1)

    g2 = swap(payload, "grp", 2)
    parts = [stack(p0[j], p1[j * rows : (j + 1) * rows], p2[j]) for j in range(4)]
    parts_there = [to_core(p) for p in parts]
    acts = []
    for side in (parts, parts_there):
        pre = 0.0
        for j, part in enumerate(side):
            w_part = lax.dynamic_slice_in_dim(in_weights, (place ^ j) * quarter, quarter, 1)
            pre = pre + lax.dot_general(w_part, part, contract_last, **wide)
        acts.append(activate(pre))
    values = phase(beside(*(a[0] for a in acts)), payload, down_weight, *parts, *parts_there)
    hidden, payload, down_weight, parts, parts_there = values[0], values[1], values[2], values[3:7], values[7:]

    hx, hy = swap(hidden, "dp", 1), swap(hidden, "dp", 2)
    down_rows, payload = phase(regroup(down_weight[0], 0, place), payload)
    g1, g3 = swap(payload, "grp", 1), swap(payload, "grp", 3)
    hx, hy, g1, g3 = phase(hx, hy, g1, g3)
    blocks = jnp.stack([payload, g1, g2, g3])
    last_x, last_y = swap(hy[half:], "dp", 1), swap(hx[:half], "dp", 2)
    blocks = stack(blocks, to_core(blocks))
    table = blocks[:, rows:, :rows].astype(wide_type).reshape(8, 2, experts, rows)
    scale = lax.dynamic_index_in_dim(table, expert, 2, keepdims=False)
    scale = jnp.sum(scale, axis=1).reshape(8 * rows, 1)
    grads = blocks[:, :rows].reshape(8 * rows, quarter).astype(wide_type)
    grads = (grads * scale).astype(half_type)
    shares = lax.dot_general(down_rows, grads, contract_last, **wide).reshape(4, units, -1)
    sent = shares[3].astype(half_type)
    top, bottom = swap(sent[:half], "dp", 2), swap(sent[half:], "dp", 1)
    sums = [
        stack(shares[1][:half] + top.astype(wide_type), shares[1][half:]).astype(half_type),
        stack(shares[2][:half], shares[2][half:] + bottom.astype(wide_type)).astype(half_type),
    ]
    sums = [swap(value, "dp", j + 1) for j, value in enumerate(sums)]
    own_share, *hidden = phase(shares[0], hidden, hx, hy, last_y, last_x)
    hidden = stack(*hidden)

    out = [
        lax.dot_general(hidden[:, k * 4 * rows : (k + 1) * 4 * rows], down_rows, contract_first, **wide)
        .astype(half_type)
        .astype(wide_type)
        * scale[k * 4 * rows : (k + 1) * 4 * rows]
        for k in range(2)
    ]
    out, hidden, grads = phase(out[0] + to_core(out[1].astype(half_type)).astype(wide_type), hidden, grads)
    back = out[rows:].astype(half_type)
    back = [swap(back[k * rows : (k + 1) * rows], "grp", k + 1) for k in (1, 0, 2)]
    total, *sums = phase(out[:rows], *sums)
    layer_out = total + back[0].astype(wide_type) + back[1].astype(wide_type) + back[2].astype(wide_type)
    down_gradient = jnp.dot(hidden, grads, **wide)
    down_gradient = regroup(down_gradient.astype(half_type), 0, place)

    factors = [f for a in acts for f in a[1:]]
    gate_gradient, up_gradient = in_gradients(
        place.reshape(1).astype(jnp.int32), own_share, sums, factors, parts, parts_there
    )
    return (layer_out.astype(half_type), gate_gradient[None], up_gradient[None], down_gradient[None])


def body(tokens, grad_out, expert_ids, *rest):
    experts = lax.axis_size(("grp", "loc"))
    rows, per_token = expert_ids.shape
    square = lax.axis_size("dp") == 4 and lax.axis_size("grp") == 4 and lax.axis_size("loc") == 2
    if square and 2 * rows * per_token // experts >= rows:
        return dense_body(tokens, grad_out, expert_ids, *rest)
    return slot_body(tokens, grad_out, expert_ids, *rest)


def solution(mesh):
    return jax.shard_map(
        body,
        mesh=mesh,
        in_specs=(
            P(("grp", "loc"), "dp"),
            P(("grp", "loc"), "dp"),
            P(("grp", "loc"), None),
            P(("grp", "loc"), None),
            P(("grp", "loc"), "dp", None),
            P(("grp", "loc"), "dp", None),
            P(("grp", "loc"), None, "dp"),
        ),
        out_specs=(
            P(("grp", "loc"), "dp"),
            P(("grp", "loc"), "dp", None),
            P(("grp", "loc"), "dp", None),
            P(("grp", "loc"), None, "dp"),
        ),
        check_vma=False,
    )
```

```python
import jax
import jax.numpy as jnp
from jax import lax
from jax.experimental import pallas as pl
from jax.experimental.pallas import tpu as pltpu
from jax.sharding import PartitionSpec as P


def slot_layout(route_ids, experts, capacity):
    flat_ids = route_ids.reshape(-1)
    onehot = (
        flat_ids[:, None] == lax.broadcasted_iota(jnp.int32, (flat_ids.shape[0], experts), 1)
    ).astype(jnp.int32)
    ranks = jnp.sum((jnp.cumsum(onehot, axis=0) - 1) * onehot, axis=1)
    return flat_ids * capacity + ranks


def place_matrix(positions, tok_rows, per_token, slots_total):
    slot_index = lax.broadcasted_iota(jnp.int32, (slots_total, tok_rows, per_token), 0)
    hits = slot_index == positions.reshape(1, tok_rows, per_token)
    return jnp.sum(hits.astype(jnp.float32), axis=2).astype(jnp.bfloat16)


def send_rows(outgoing):
    return lax.all_to_all(outgoing, ("grp", "loc"), split_axis=0, concat_axis=0, tiled=True)


def return_rows(results):
    return lax.all_to_all(results, ("grp", "loc"), split_axis=0, concat_axis=0, tiled=True)


def slot_body(tokens, grad_out, expert_ids, gate_scale, gate_weight, up_weight, down_weight):
    tok_rows, quarter = tokens.shape
    per_token = expert_ids.shape[1]
    experts = lax.axis_size(("grp", "loc"))
    capacity = min(tok_rows, max(2, 2 * tok_rows * per_token // experts))
    slots_total = experts * capacity
    positions = slot_layout(expert_ids, experts, capacity)
    unit_place = place_matrix(positions, tok_rows, per_token, slots_total)
    slot_scale = jnp.zeros((slots_total,), jnp.float32).at[positions].set(gate_scale.reshape(-1))
    picked_grads = jnp.dot(unit_place, grad_out, preferred_element_type=jnp.float32)
    grad_rows = (picked_grads * slot_scale[:, None]).astype(jnp.bfloat16)
    full_tokens = lax.all_gather(tokens, "dp", axis=1, tiled=True)
    features = full_tokens.shape[1]
    token_rows = jnp.dot(unit_place, full_tokens, preferred_element_type=jnp.float32).astype(
        jnp.bfloat16
    )
    outgoing = jnp.concatenate([token_rows, grad_rows], axis=1).reshape(
        experts, capacity, features + quarter
    )
    arrived = send_rows(outgoing)
    slot_tokens = arrived[:, :, :features]
    slot_grads = arrived[:, :, features:]
    flat_tokens = slot_tokens.reshape(slots_total, -1)
    flat_grads = slot_grads.reshape(slots_total, quarter)
    gate_mat = gate_weight[0]
    up_mat = up_weight[0]
    down_mat = down_weight[0]
    feature_contract = (((1,), (1,)), ((), ()))
    gate_pre = lax.dot_general(
        gate_mat, flat_tokens, feature_contract, preferred_element_type=jnp.float32
    )
    up_pre = lax.dot_general(
        up_mat, flat_tokens, feature_contract, preferred_element_type=jnp.float32
    )
    sigmoid_gate = jax.nn.sigmoid(gate_pre)
    activated = gate_pre * sigmoid_gate
    hidden = (activated * up_pre).astype(jnp.bfloat16)
    piece = lax.all_gather(hidden, "dp", axis=0, tiled=True)
    down_rows = down_mat
    out_total = lax.dot_general(
        piece, down_rows, (((0,), (0,)), ((), ())), preferred_element_type=jnp.float32
    )
    block_grad = jnp.dot(piece, flat_grads, preferred_element_type=jnp.float32)
    down_total = block_grad
    out_total, down_total = (out_total, down_total)
    expert_out = out_total.astype(jnp.bfloat16)
    down_gradient = down_total.astype(jnp.bfloat16)
    returned = return_rows(expert_out.reshape(experts, capacity, quarter)).reshape(
        slots_total, quarter
    )
    picked = returned[positions].astype(jnp.float32) * gate_scale.reshape(-1)[:, None]
    layer_out = jnp.sum(picked.reshape(tok_rows, per_token, quarter), axis=1).astype(jnp.bfloat16)
    down_rows = down_mat
    hidden_grad = lax.psum_scatter(
        lax.dot_general(
            down_rows, flat_grads, feature_contract, preferred_element_type=jnp.float32
        ),
        "dp",
        scatter_dimension=0,
        tiled=True,
    )
    gate_grad = (
        hidden_grad * up_pre * sigmoid_gate * (1.0 + gate_pre * (1.0 - sigmoid_gate))
    ).astype(jnp.bfloat16)
    up_grad = (hidden_grad * activated).astype(jnp.bfloat16)
    gate_gradient = jnp.dot(gate_grad, flat_tokens, preferred_element_type=jnp.float32).astype(
        jnp.bfloat16
    )
    up_gradient = jnp.dot(up_grad, flat_tokens, preferred_element_type=jnp.float32).astype(
        jnp.bfloat16
    )
    return (layer_out, gate_gradient[None], up_gradient[None], down_gradient[None])


def swap(value, axis, bit):
    pairs = [(i, i ^ bit) for i in range(lax.axis_size(axis))]
    return lax.ppermute(value, axis, pairs)


def spread(value):
    return [swap(value, "dp", j) for j in (1, 2, 3)]


def to_core(value):
    return swap(value, "loc", 1)


def stack(*values):
    return jnp.concatenate(values, axis=0)


def beside(*values):
    return jnp.concatenate(values, axis=1)


def phase(*values):
    return lax.optimization_barrier(values)


def regroup(value, axis, place):
    size = value.shape[axis] // 4
    return jnp.concatenate(
        [lax.dynamic_slice_in_dim(value, (place ^ j) * size, size, axis) for j in range(4)], axis=axis
    )


def activate(pre):
    units = pre.shape[0] // 2
    gate_pre, up_pre = pre[:units], pre[units:]
    sig = jax.nn.sigmoid(gate_pre)
    activated = gate_pre * sig
    return (activated * up_pre).astype(jnp.bfloat16), up_pre * sig * (1.0 + gate_pre * (1.0 - sig)), activated


def in_gradients(place, own_share, sums, factors, parts, parts_there):
    units, width = factors[0].shape
    quarter = parts[0].shape[1]

    def kernel(place_ref, share_ref, x_ref, y_ref, *refs):
        factor_refs, part_refs, (gate_ref, up_ref) = refs[:4], refs[4:12], refs[12:]
        total = share_ref[...] + x_ref[...].astype(jnp.float32) + y_ref[...].astype(jnp.float32)
        sides = []
        for k in range(2):
            side = total[:, k * width : (k + 1) * width]
            sides.append([(side * factor_refs[2 * k + i][...]).astype(jnp.bfloat16) for i in range(2)])
        for j in range(4):
            columns = pl.ds(pl.multiple_of((place_ref[0] ^ j) * quarter, quarter), quarter)
            for i, out_ref in enumerate((gate_ref, up_ref)):
                value = jnp.dot(sides[0][i], part_refs[j][...], preferred_element_type=jnp.float32)
                value += jnp.dot(sides[1][i], part_refs[4 + j][...], preferred_element_type=jnp.float32)
                out_ref[:, columns] = value.astype(jnp.bfloat16)

    vmem = pl.BlockSpec(memory_space=pltpu.VMEM)
    return pl.pallas_call(
        kernel,
        out_shape=[jax.ShapeDtypeStruct((units, 4 * quarter), jnp.bfloat16)] * 2,
        in_specs=[pl.BlockSpec(memory_space=pltpu.SMEM)] + [vmem] * 15,
        out_specs=[vmem] * 2,
        compiler_params=pltpu.CompilerParams(vmem_limit_bytes=20 * 2**20),
    )(place, own_share, *sums, *factors, *parts, *parts_there)


def dense_body(tokens, grad_out, expert_ids, gate_scale, gate_weight, up_weight, down_weight):
    rows, quarter = tokens.shape
    experts = lax.axis_size(("grp", "loc"))
    place = lax.axis_index("dp")
    expert = lax.axis_index(("grp", "loc"))
    units = gate_weight.shape[1]
    half = units // 2
    contract_last = (((1,), (1,)), ((), ()))
    contract_first = (((0,), (0,)), ((), ()))
    wide = dict(preferred_element_type=jnp.float32)
    half_type, wide_type = jnp.bfloat16, jnp.float32

    t2, t3 = swap(tokens, "grp", 2), swap(tokens, "grp", 3)
    p0 = [tokens] + spread(tokens)
    in_weights = stack(gate_weight[0], up_weight[0])
    named = lax.broadcasted_iota(jnp.int32, (experts, rows, 1), 0) == expert_ids[None]
    scales = jnp.sum(jnp.where(named, gate_scale[None], 0.0), axis=2)
    high = lax.reduce_precision(scales, 8, 7)
    table = stack(high, scales - high).astype(half_type)
    table = jnp.pad(table, ((0, 0), (0, quarter - rows)))
    payload = stack(grad_out, table)
    own = stack(*p0)
    p1 = swap(own, "grp", 1)
    own, far, payload, in_weights = phase(own, stack(t2, t3), payload, in_weights)
    p0 = [own[j * rows : (j + 1) * rows] for j in range(4)]

    p2 = [far] + spread(far)
    late, p1 = phase(payload, p1)
    g2, g3 = swap(late, "grp", 2), swap(late, "grp", 3)
    *p2, payload, p1 = phase(*p2, payload, p1)

    parts = [stack(p0[j], p1[j * rows : (j + 1) * rows], p2[j]) for j in range(4)]
    parts_there = [to_core(p) for p in parts]
    acts = []
    for side in (parts, parts_there):
        pre = 0.0
        for j, part in enumerate(side):
            w_part = lax.dynamic_slice_in_dim(in_weights, (place ^ j) * quarter, quarter, 1)
            pre = pre + lax.dot_general(w_part, part, contract_last, **wide)
        acts.append(activate(pre))
    values = phase(beside(*(a[0] for a in acts)), payload, down_weight, *parts, *parts_there)
    hidden, payload, down_weight, parts, parts_there = values[0], values[1], values[2], values[3:7], values[7:]

    hx, hy = swap(hidden, "dp", 1), swap(hidden, "dp", 2)
    down_rows, payload = phase(regroup(down_weight[0], 0, place), payload)
    g1 = swap(payload, "grp", 1)
    last_x, last_y = swap(hy[half:], "dp", 1), swap(hx[:half], "dp", 2)
    blocks = jnp.stack([payload, g1, g2, g3])
    blocks = stack(blocks, to_core(blocks))
    table = blocks[:, rows:, :rows].astype(wide_type).reshape(8, 2, experts, rows)
    scale = lax.dynamic_index_in_dim(table, expert, 2, keepdims=False)
    scale = jnp.sum(scale, axis=1).reshape(8 * rows, 1)
    grads = blocks[:, :rows].reshape(8 * rows, quarter).astype(wide_type)
    grads = (grads * scale).astype(half_type)
    shares = lax.dot_general(down_rows, grads, contract_last, **wide).reshape(4, units, -1)
    sent = shares[3].astype(half_type)
    top, bottom = swap(sent[:half], "dp", 2), swap(sent[half:], "dp", 1)
    sums = [
        stack(shares[1][:half] + top.astype(wide_type), shares[1][half:]).astype(half_type),
        stack(shares[2][:half], shares[2][half:] + bottom.astype(wide_type)).astype(half_type),
    ]
    sums = [swap(value, "dp", j + 1) for j, value in enumerate(sums)]
    own_share, *hidden = phase(shares[0], hidden, hx, hy, last_y, last_x)
    hidden = stack(*hidden)

    out = [
        lax.dot_general(hidden[:, k * 4 * rows : (k + 1) * 4 * rows], down_rows, contract_first, **wide)
        .astype(half_type)
        .astype(wide_type)
        * scale[k * 4 * rows : (k + 1) * 4 * rows]
        for k in range(2)
    ]
    out, hidden, grads = phase(out[0] + to_core(out[1].astype(half_type)).astype(wide_type), hidden, grads)
    back = out[rows:].astype(half_type)
    back = [swap(back[k * rows : (k + 1) * rows], "grp", k + 1) for k in (1, 0, 2)]
    total, *sums = phase(out[:rows], *sums)
    layer_out = total + back[0].astype(wide_type) + back[1].astype(wide_type) + back[2].astype(wide_type)
    down_gradient = jnp.dot(hidden, grads, **wide)
    down_gradient = regroup(down_gradient.astype(half_type), 0, place)

    factors = [f for a in acts for f in a[1:]]
    gate_gradient, up_gradient = in_gradients(
        place.reshape(1).astype(jnp.int32), own_share, sums, factors, parts, parts_there
    )
    return (layer_out.astype(half_type), gate_gradient[None], up_gradient[None], down_gradient[None])


def body(tokens, grad_out, expert_ids, *rest):
    experts = lax.axis_size(("grp", "loc"))
    rows, per_token = expert_ids.shape
    square = lax.axis_size("dp") == 4 and lax.axis_size("grp") == 4 and lax.axis_size("loc") == 2
    if square and 2 * rows * per_token // experts >= rows:
        return dense_body(tokens, grad_out, expert_ids, *rest)
    return slot_body(tokens, grad_out, expert_ids, *rest)


def solution(mesh):
    return jax.shard_map(
        body,
        mesh=mesh,
        in_specs=(
            P(("grp", "loc"), "dp"),
            P(("grp", "loc"), "dp"),
            P(("grp", "loc"), None),
            P(("grp", "loc"), None),
            P(("grp", "loc"), "dp", None),
            P(("grp", "loc"), "dp", None),
            P(("grp", "loc"), None, "dp"),
        ),
        out_specs=(
            P(("grp", "loc"), "dp"),
            P(("grp", "loc"), "dp", None),
            P(("grp", "loc"), "dp", None),
            P(("grp", "loc"), None, "dp"),
        ),
        check_vma=False,
    )
```

```python
import jax
import jax.numpy as jnp
from jax import lax
from jax.experimental import pallas as pl
from jax.experimental.pallas import tpu as pltpu
from jax.sharding import PartitionSpec as P


def slot_layout(route_ids, experts, capacity):
    flat_ids = route_ids.reshape(-1)
    onehot = (
        flat_ids[:, None] == lax.broadcasted_iota(jnp.int32, (flat_ids.shape[0], experts), 1)
    ).astype(jnp.int32)
    ranks = jnp.sum((jnp.cumsum(onehot, axis=0) - 1) * onehot, axis=1)
    return flat_ids * capacity + ranks


def place_matrix(positions, tok_rows, per_token, slots_total):
    slot_index = lax.broadcasted_iota(jnp.int32, (slots_total, tok_rows, per_token), 0)
    hits = slot_index == positions.reshape(1, tok_rows, per_token)
    return jnp.sum(hits.astype(jnp.float32), axis=2).astype(jnp.bfloat16)


def send_rows(outgoing):
    return lax.all_to_all(outgoing, ("grp", "loc"), split_axis=0, concat_axis=0, tiled=True)


def return_rows(results):
    return lax.all_to_all(results, ("grp", "loc"), split_axis=0, concat_axis=0, tiled=True)


def slot_body(tokens, grad_out, expert_ids, gate_scale, gate_weight, up_weight, down_weight):
    tok_rows, quarter = tokens.shape
    per_token = expert_ids.shape[1]
    experts = lax.axis_size(("grp", "loc"))
    capacity = min(tok_rows, max(2, 2 * tok_rows * per_token // experts))
    slots_total = experts * capacity
    positions = slot_layout(expert_ids, experts, capacity)
    unit_place = place_matrix(positions, tok_rows, per_token, slots_total)
    slot_scale = jnp.zeros((slots_total,), jnp.float32).at[positions].set(gate_scale.reshape(-1))
    picked_grads = jnp.dot(unit_place, grad_out, preferred_element_type=jnp.float32)
    grad_rows = (picked_grads * slot_scale[:, None]).astype(jnp.bfloat16)
    full_tokens = lax.all_gather(tokens, "dp", axis=1, tiled=True)
    features = full_tokens.shape[1]
    token_rows = jnp.dot(unit_place, full_tokens, preferred_element_type=jnp.float32).astype(
        jnp.bfloat16
    )
    outgoing = jnp.concatenate([token_rows, grad_rows], axis=1).reshape(
        experts, capacity, features + quarter
    )
    arrived = send_rows(outgoing)
    slot_tokens = arrived[:, :, :features]
    slot_grads = arrived[:, :, features:]
    flat_tokens = slot_tokens.reshape(slots_total, -1)
    flat_grads = slot_grads.reshape(slots_total, quarter)
    gate_mat = gate_weight[0]
    up_mat = up_weight[0]
    down_mat = down_weight[0]
    feature_contract = (((1,), (1,)), ((), ()))
    gate_pre = lax.dot_general(
        gate_mat, flat_tokens, feature_contract, preferred_element_type=jnp.float32
    )
    up_pre = lax.dot_general(
        up_mat, flat_tokens, feature_contract, preferred_element_type=jnp.float32
    )
    sigmoid_gate = jax.nn.sigmoid(gate_pre)
    activated = gate_pre * sigmoid_gate
    hidden = (activated * up_pre).astype(jnp.bfloat16)
    piece = lax.all_gather(hidden, "dp", axis=0, tiled=True)
    down_rows = down_mat
    out_total = lax.dot_general(
        piece, down_rows, (((0,), (0,)), ((), ())), preferred_element_type=jnp.float32
    )
    block_grad = jnp.dot(piece, flat_grads, preferred_element_type=jnp.float32)
    down_total = block_grad
    out_total, down_total = (out_total, down_total)
    expert_out = out_total.astype(jnp.bfloat16)
    down_gradient = down_total.astype(jnp.bfloat16)
    returned = return_rows(expert_out.reshape(experts, capacity, quarter)).reshape(
        slots_total, quarter
    )
    picked = returned[positions].astype(jnp.float32) * gate_scale.reshape(-1)[:, None]
    layer_out = jnp.sum(picked.reshape(tok_rows, per_token, quarter), axis=1).astype(jnp.bfloat16)
    down_rows = down_mat
    hidden_grad = lax.psum_scatter(
        lax.dot_general(
            down_rows, flat_grads, feature_contract, preferred_element_type=jnp.float32
        ),
        "dp",
        scatter_dimension=0,
        tiled=True,
    )
    gate_grad = (
        hidden_grad * up_pre * sigmoid_gate * (1.0 + gate_pre * (1.0 - sigmoid_gate))
    ).astype(jnp.bfloat16)
    up_grad = (hidden_grad * activated).astype(jnp.bfloat16)
    gate_gradient = jnp.dot(gate_grad, flat_tokens, preferred_element_type=jnp.float32).astype(
        jnp.bfloat16
    )
    up_gradient = jnp.dot(up_grad, flat_tokens, preferred_element_type=jnp.float32).astype(
        jnp.bfloat16
    )
    return (layer_out, gate_gradient[None], up_gradient[None], down_gradient[None])


def swap(value, axis, bit):
    pairs = [(i, i ^ bit) for i in range(lax.axis_size(axis))]
    return lax.ppermute(value, axis, pairs)


def spread(value):
    return [swap(value, "dp", j) for j in (1, 2, 3)]


def to_core(value):
    return swap(value, "loc", 1)


def stack(*values):
    return jnp.concatenate(values, axis=0)


def beside(*values):
    return jnp.concatenate(values, axis=1)


def phase(*values):
    return lax.optimization_barrier(values)


def regroup(value, axis, place):
    size = value.shape[axis] // 4
    return jnp.concatenate(
        [lax.dynamic_slice_in_dim(value, (place ^ j) * size, size, axis) for j in range(4)], axis=axis
    )


def activate(pre):
    units = pre.shape[0] // 2
    gate_pre, up_pre = pre[:units], pre[units:]
    sig = jax.nn.sigmoid(gate_pre)
    activated = gate_pre * sig
    return (activated * up_pre).astype(jnp.bfloat16), up_pre * sig * (1.0 + gate_pre * (1.0 - sig)), activated


def in_gradients(place, own_share, sums, factors, sides):
    units, width = factors[0].shape
    quarter = sides[0][0].shape[1]
    rows = sides[0][0].shape[0] // 4

    def kernel(place_ref, share_ref, x_ref, y_ref, *refs):
        factor_refs, side_refs, (gate_ref, up_ref) = refs[:4], (refs[4:10], refs[10:16]), refs[16:]
        total = share_ref[...] + x_ref[...].astype(jnp.float32) + y_ref[...].astype(jnp.float32)
        lefts = []
        for k in range(2):
            side = total[:, k * width : (k + 1) * width]
            lefts.append([(side * factor_refs[2 * k + i][...]).astype(jnp.bfloat16) for i in range(2)])
        for j in range(4):
            columns = pl.ds(pl.multiple_of((place_ref[0] ^ j) * quarter, quarter), quarter)
            rights = []
            for own_ref, near_ref, *far_refs in side_refs:
                block = pl.ds(j * rows, rows)
                rights.append(jnp.concatenate([own_ref[block], near_ref[block], far_refs[j][...]], axis=0))
            for i, out_ref in enumerate((gate_ref, up_ref)):
                value = jnp.dot(lefts[0][i], rights[0], preferred_element_type=jnp.float32)
                value += jnp.dot(lefts[1][i], rights[1], preferred_element_type=jnp.float32)
                out_ref[:, columns] = value.astype(jnp.bfloat16)

    vmem = pl.BlockSpec(memory_space=pltpu.VMEM)
    return pl.pallas_call(
        kernel,
        out_shape=[jax.ShapeDtypeStruct((units, 4 * quarter), jnp.bfloat16)] * 2,
        in_specs=[pl.BlockSpec(memory_space=pltpu.SMEM)] + [vmem] * 19,
        out_specs=[vmem] * 2,
        compiler_params=pltpu.CompilerParams(vmem_limit_bytes=20 * 2**20),
    )(place, own_share, *sums, *factors, *sides[0], *sides[1])


def dense_body(tokens, grad_out, expert_ids, gate_scale, gate_weight, up_weight, down_weight):
    rows, quarter = tokens.shape
    experts = lax.axis_size(("grp", "loc"))
    place = lax.axis_index("dp")
    expert = lax.axis_index(("grp", "loc"))
    units = gate_weight.shape[1]
    half = units // 2
    contract_last = (((1,), (1,)), ((), ()))
    contract_first = (((0,), (0,)), ((), ()))
    wide = dict(preferred_element_type=jnp.float32)
    half_type, wide_type = jnp.bfloat16, jnp.float32

    def dot_part(weights, j, part):
        weights = lax.dynamic_slice_in_dim(weights, (place ^ j) * quarter, quarter, 1)
        return lax.dot_general(weights, part, contract_last, **wide)

    def block_part(weights, block):
        return sum(dot_part(weights, j, block[j * rows : (j + 1) * rows]) for j in range(4))

    t2, t3 = swap(tokens, "grp", 2), swap(tokens, "grp", 3)
    p0 = [tokens] + spread(tokens)
    in_weights = stack(gate_weight[0], up_weight[0])
    named = lax.broadcasted_iota(jnp.int32, (experts, rows, 1), 0) == expert_ids[None]
    scales = jnp.sum(jnp.where(named, gate_scale[None], 0.0), axis=2)
    high = lax.reduce_precision(scales, 8, 7)
    table = stack(high, scales - high).astype(half_type)
    table = jnp.pad(table, ((0, 0), (0, quarter - rows)))
    payload = stack(grad_out, table)
    own = stack(*p0)
    p1 = swap(own, "grp", 1)
    own, far, payload, in_weights, *p0 = phase(own, stack(t2, t3), payload, in_weights, *p0)
    own_there, far_there = to_core(own), to_core(far)
    pre_own = [block_part(in_weights, block) for block in (own, own_there)]
    pre_far = [dot_part(in_weights, 0, block) for block in (far, far_there)]

    p2 = [far] + spread(far)
    late, own_there = phase(payload, own_there)
    g3 = swap(late, "grp", 3)
    late, p1 = phase(payload, p1)
    g2 = swap(late, "grp", 2)
    p1_there = to_core(p1)
    pre_near = [block_part(in_weights, block) for block in (p1, p1_there)]
    values = phase(*p2, payload, p1, p1_there, far_there, *pre_far, *pre_own, *pre_near)
    p2, (payload, p1, p1_there, far_there), pre_far = values[:4], values[4:8], list(values[8:10])
    pre_own, pre_near = values[10:12], values[12:]

    p2_there = [far_there] + [to_core(block) for block in p2[1:]]
    acts = []
    for k, (near, far_parts) in enumerate(((p1, p2), (p1_there, p2_there))):
        for j in (1, 2, 3):
            pre_far[k] = pre_far[k] + dot_part(in_weights, j, far_parts[j])
        acts.append([activate(pre) for pre in (pre_own[k], pre_near[k], pre_far[k])])
    sides = ((own, p1, *p2), (own_there, p1_there, *p2_there))
    hidden, payload, down_weight, *values = phase(
        beside(*(a[0] for side in acts for a in side)), payload, down_weight, *sides[0], *sides[1]
    )
    sides = (values[:6], values[6:])

    hx, hy = swap(hidden, "dp", 1), swap(hidden, "dp", 2)
    down_rows, payload = phase(regroup(down_weight[0], 0, place), payload)
    g1 = swap(payload, "grp", 1)
    last_x, last_y = swap(hy[half:], "dp", 1), swap(hx[:half], "dp", 2)
    blocks = jnp.stack([payload, g1, g2, g3])
    blocks = stack(blocks, to_core(blocks))
    table = blocks[:, rows:, :rows].astype(wide_type).reshape(8, 2, experts, rows)
    scale = lax.dynamic_index_in_dim(table, expert, 2, keepdims=False)
    scale = jnp.sum(scale, axis=1).reshape(8 * rows, 1)
    grads = blocks[:, :rows].reshape(8 * rows, quarter).astype(wide_type)
    grads = (grads * scale).astype(half_type)
    shares = lax.dot_general(down_rows, grads, contract_last, **wide).reshape(4, units, -1)
    sent = shares[3].astype(half_type)
    top, bottom = swap(sent[:half], "dp", 2), swap(sent[half:], "dp", 1)
    sums = [
        stack(shares[1][:half] + top.astype(wide_type), shares[1][half:]).astype(half_type),
        stack(shares[2][:half], shares[2][half:] + bottom.astype(wide_type)).astype(half_type),
    ]
    sums = [swap(value, "dp", j + 1) for j, value in enumerate(sums)]
    own_share, *hidden = phase(shares[0], hidden, hx, hy, last_y, last_x)
    hidden = stack(*hidden)

    out = [
        lax.dot_general(hidden[:, k * 4 * rows : (k + 1) * 4 * rows], down_rows, contract_first, **wide)
        .astype(half_type)
        .astype(wide_type)
        * scale[k * 4 * rows : (k + 1) * 4 * rows]
        for k in range(2)
    ]
    out, hidden, grads = phase(out[0] + to_core(out[1].astype(half_type)).astype(wide_type), hidden, grads)
    back = out[rows:].astype(half_type)
    back = [swap(back[k * rows : (k + 1) * rows], "grp", k + 1) for k in (1, 0, 2)]
    total, *sums = phase(out[:rows], *sums)
    layer_out = total + back[0].astype(wide_type) + back[1].astype(wide_type) + back[2].astype(wide_type)
    down_gradient = jnp.dot(hidden, grads, **wide)
    down_gradient = regroup(down_gradient.astype(half_type), 0, place)

    factors = [beside(*(a[i] for a in side)) for side in acts for i in (1, 2)]
    gate_gradient, up_gradient = in_gradients(
        place.reshape(1).astype(jnp.int32), own_share, sums, factors, sides
    )
    return (layer_out.astype(half_type), gate_gradient[None], up_gradient[None], down_gradient[None])


def body(tokens, grad_out, expert_ids, *rest):
    experts = lax.axis_size(("grp", "loc"))
    rows, per_token = expert_ids.shape
    square = lax.axis_size("dp") == 4 and lax.axis_size("grp") == 4 and lax.axis_size("loc") == 2
    if square and 2 * rows * per_token // experts >= rows:
        return dense_body(tokens, grad_out, expert_ids, *rest)
    return slot_body(tokens, grad_out, expert_ids, *rest)


def solution(mesh):
    return jax.shard_map(
        body,
        mesh=mesh,
        in_specs=(
            P(("grp", "loc"), "dp"),
            P(("grp", "loc"), "dp"),
            P(("grp", "loc"), None),
            P(("grp", "loc"), None),
            P(("grp", "loc"), "dp", None),
            P(("grp", "loc"), "dp", None),
            P(("grp", "loc"), None, "dp"),
        ),
        out_specs=(
            P(("grp", "loc"), "dp"),
            P(("grp", "loc"), "dp", None),
            P(("grp", "loc"), "dp", None),
            P(("grp", "loc"), None, "dp"),
        ),
        check_vma=False,
    )
```

```python
import jax
import jax.numpy as jnp
from jax import lax
from jax.experimental import pallas as pl
from jax.experimental.pallas import tpu as pltpu
from jax.sharding import PartitionSpec as P


def slot_layout(route_ids, experts, capacity):
    flat_ids = route_ids.reshape(-1)
    onehot = (
        flat_ids[:, None] == lax.broadcasted_iota(jnp.int32, (flat_ids.shape[0], experts), 1)
    ).astype(jnp.int32)
    ranks = jnp.sum((jnp.cumsum(onehot, axis=0) - 1) * onehot, axis=1)
    return flat_ids * capacity + ranks


def place_matrix(positions, tok_rows, per_token, slots_total):
    slot_index = lax.broadcasted_iota(jnp.int32, (slots_total, tok_rows, per_token), 0)
    hits = slot_index == positions.reshape(1, tok_rows, per_token)
    return jnp.sum(hits.astype(jnp.float32), axis=2).astype(jnp.bfloat16)


def send_rows(outgoing):
    return lax.all_to_all(outgoing, ("grp", "loc"), split_axis=0, concat_axis=0, tiled=True)


def return_rows(results):
    return lax.all_to_all(results, ("grp", "loc"), split_axis=0, concat_axis=0, tiled=True)


def slot_body(tokens, grad_out, expert_ids, gate_scale, gate_weight, up_weight, down_weight):
    tok_rows, quarter = tokens.shape
    per_token = expert_ids.shape[1]
    experts = lax.axis_size(("grp", "loc"))
    capacity = min(tok_rows, max(2, 2 * tok_rows * per_token // experts))
    slots_total = experts * capacity
    positions = slot_layout(expert_ids, experts, capacity)
    unit_place = place_matrix(positions, tok_rows, per_token, slots_total)
    slot_scale = jnp.zeros((slots_total,), jnp.float32).at[positions].set(gate_scale.reshape(-1))
    picked_grads = jnp.dot(unit_place, grad_out, preferred_element_type=jnp.float32)
    grad_rows = (picked_grads * slot_scale[:, None]).astype(jnp.bfloat16)
    full_tokens = lax.all_gather(tokens, "dp", axis=1, tiled=True)
    features = full_tokens.shape[1]
    token_rows = jnp.dot(unit_place, full_tokens, preferred_element_type=jnp.float32).astype(
        jnp.bfloat16
    )
    outgoing = jnp.concatenate([token_rows, grad_rows], axis=1).reshape(
        experts, capacity, features + quarter
    )
    arrived = send_rows(outgoing)
    slot_tokens = arrived[:, :, :features]
    slot_grads = arrived[:, :, features:]
    flat_tokens = slot_tokens.reshape(slots_total, -1)
    flat_grads = slot_grads.reshape(slots_total, quarter)
    gate_mat = gate_weight[0]
    up_mat = up_weight[0]
    down_mat = down_weight[0]
    feature_contract = (((1,), (1,)), ((), ()))
    gate_pre = lax.dot_general(
        gate_mat, flat_tokens, feature_contract, preferred_element_type=jnp.float32
    )
    up_pre = lax.dot_general(
        up_mat, flat_tokens, feature_contract, preferred_element_type=jnp.float32
    )
    sigmoid_gate = jax.nn.sigmoid(gate_pre)
    activated = gate_pre * sigmoid_gate
    hidden = (activated * up_pre).astype(jnp.bfloat16)
    piece = lax.all_gather(hidden, "dp", axis=0, tiled=True)
    down_rows = down_mat
    out_total = lax.dot_general(
        piece, down_rows, (((0,), (0,)), ((), ())), preferred_element_type=jnp.float32
    )
    block_grad = jnp.dot(piece, flat_grads, preferred_element_type=jnp.float32)
    down_total = block_grad
    out_total, down_total = (out_total, down_total)
    expert_out = out_total.astype(jnp.bfloat16)
    down_gradient = down_total.astype(jnp.bfloat16)
    returned = return_rows(expert_out.reshape(experts, capacity, quarter)).reshape(
        slots_total, quarter
    )
    picked = returned[positions].astype(jnp.float32) * gate_scale.reshape(-1)[:, None]
    layer_out = jnp.sum(picked.reshape(tok_rows, per_token, quarter), axis=1).astype(jnp.bfloat16)
    down_rows = down_mat
    hidden_grad = lax.psum_scatter(
        lax.dot_general(
            down_rows, flat_grads, feature_contract, preferred_element_type=jnp.float32
        ),
        "dp",
        scatter_dimension=0,
        tiled=True,
    )
    gate_grad = (
        hidden_grad * up_pre * sigmoid_gate * (1.0 + gate_pre * (1.0 - sigmoid_gate))
    ).astype(jnp.bfloat16)
    up_grad = (hidden_grad * activated).astype(jnp.bfloat16)
    gate_gradient = jnp.dot(gate_grad, flat_tokens, preferred_element_type=jnp.float32).astype(
        jnp.bfloat16
    )
    up_gradient = jnp.dot(up_grad, flat_tokens, preferred_element_type=jnp.float32).astype(
        jnp.bfloat16
    )
    return (layer_out, gate_gradient[None], up_gradient[None], down_gradient[None])


def swap(value, axis, bit):
    pairs = [(i, i ^ bit) for i in range(lax.axis_size(axis))]
    return lax.ppermute(value, axis, pairs)


def spread(value):
    return [swap(value, "dp", j) for j in (1, 2, 3)]


def to_core(value):
    return swap(value, "loc", 1)


def stack(*values):
    return jnp.concatenate(values, axis=0)


def beside(*values):
    return jnp.concatenate(values, axis=1)


def phase(*values):
    return lax.optimization_barrier(values)


def regroup(value, axis, place):
    size = value.shape[axis] // 4
    return jnp.concatenate(
        [lax.dynamic_slice_in_dim(value, (place ^ j) * size, size, axis) for j in range(4)], axis=axis
    )


def activate(pre):
    units = pre.shape[0] // 2
    gate_pre, up_pre = pre[:units], pre[units:]
    sig = jax.nn.sigmoid(gate_pre)
    activated = gate_pre * sig
    return (activated * up_pre).astype(jnp.bfloat16), up_pre * sig * (1.0 + gate_pre * (1.0 - sig)), activated


def in_gradients(place, own_share, sums, factors, sides):
    units, width = factors[0].shape
    quarter = sides[0][0].shape[1]
    rows = sides[0][0].shape[0] // 4

    def kernel(place_ref, share_ref, x_ref, y_ref, *refs):
        factor_refs, side_refs, (gate_ref, up_ref) = refs[:4], (refs[4:10], refs[10:16]), refs[16:]
        total = share_ref[...] + x_ref[...].astype(jnp.float32) + y_ref[...].astype(jnp.float32)
        lefts = []
        for k in range(2):
            side = total[:, k * width : (k + 1) * width]
            lefts.append([(side * factor_refs[2 * k + i][...]).astype(jnp.bfloat16) for i in range(2)])
        for j in range(4):
            columns = pl.ds(pl.multiple_of((place_ref[0] ^ j) * quarter, quarter), quarter)
            rights = []
            for own_ref, near_ref, *far_refs in side_refs:
                block = pl.ds(j * rows, rows)
                rights.append(jnp.concatenate([own_ref[block], near_ref[block], far_refs[j][...]], axis=0))
            for i, out_ref in enumerate((gate_ref, up_ref)):
                value = jnp.dot(lefts[0][i], rights[0], preferred_element_type=jnp.float32)
                value += jnp.dot(lefts[1][i], rights[1], preferred_element_type=jnp.float32)
                out_ref[:, columns] = value.astype(jnp.bfloat16)

    vmem = pl.BlockSpec(memory_space=pltpu.VMEM)
    return pl.pallas_call(
        kernel,
        out_shape=[jax.ShapeDtypeStruct((units, 4 * quarter), jnp.bfloat16)] * 2,
        in_specs=[pl.BlockSpec(memory_space=pltpu.SMEM)] + [vmem] * 19,
        out_specs=[vmem] * 2,
        compiler_params=pltpu.CompilerParams(vmem_limit_bytes=20 * 2**20),
    )(place, own_share, *sums, *factors, *sides[0], *sides[1])


def dense_body(tokens, grad_out, expert_ids, gate_scale, gate_weight, up_weight, down_weight):
    rows, quarter = tokens.shape
    experts = lax.axis_size(("grp", "loc"))
    place = lax.axis_index("dp")
    expert = lax.axis_index(("grp", "loc"))
    units = gate_weight.shape[1]
    half = units // 2
    contract_last = (((1,), (1,)), ((), ()))
    contract_first = (((0,), (0,)), ((), ()))
    wide = dict(preferred_element_type=jnp.float32)
    half_type, wide_type = jnp.bfloat16, jnp.float32

    def dot_part(weights, j, part):
        weights = lax.dynamic_slice_in_dim(weights, (place ^ j) * quarter, quarter, 1)
        return lax.dot_general(weights, part, contract_last, **wide)

    def block_part(weights, block):
        return sum(dot_part(weights, j, block[j * rows : (j + 1) * rows]) for j in range(4))

    t2, t3 = swap(tokens, "grp", 2), swap(tokens, "grp", 3)
    p0 = [tokens] + spread(tokens)
    in_weights = stack(gate_weight[0], up_weight[0])
    named = lax.broadcasted_iota(jnp.int32, (experts, rows, 1), 0) == expert_ids[None]
    scales = jnp.sum(jnp.where(named, gate_scale[None], 0.0), axis=2)
    high = lax.reduce_precision(scales, 8, 7)
    table = stack(high, scales - high).astype(half_type)
    table = jnp.pad(table, ((0, 0), (0, quarter - rows)))
    payload = stack(grad_out, table)
    own = stack(*p0)
    p1 = swap(own, "grp", 1)
    own, far, payload, in_weights, *p0 = phase(own, stack(t2, t3), payload, in_weights, *p0)
    own_there, far_there = to_core(own), to_core(far)
    pre_own = [block_part(in_weights, block) for block in (own, own_there)]
    pre_far = [dot_part(in_weights, 0, block) for block in (far, far_there)]

    p2 = [far] + spread(far)
    late, own_there = phase(payload, own_there)
    g3 = swap(late, "grp", 3)
    late, p1, *pre_own = phase(payload, p1, *pre_own)
    g2 = swap(late, "grp", 2)
    p1_there = to_core(p1)
    pre_near = [block_part(in_weights, block) for block in (p1, p1_there)]
    values = phase(*p2, payload, p1, p1_there, far_there, *pre_far, *pre_own, *pre_near)
    p2, (payload, p1, p1_there, far_there), pre_far = values[:4], values[4:8], list(values[8:10])
    pre_own, pre_near = values[10:12], values[12:]

    p2_there = [far_there] + [to_core(block) for block in p2[1:]]
    acts = []
    for k, (near, far_parts) in enumerate(((p1, p2), (p1_there, p2_there))):
        for j in (1, 2, 3):
            pre_far[k] = pre_far[k] + dot_part(in_weights, j, far_parts[j])
        acts.append([activate(pre) for pre in (pre_own[k], pre_near[k], pre_far[k])])
    sides = ((own, p1, *p2), (own_there, p1_there, *p2_there))
    hidden, payload, down_weight, *values = phase(
        beside(*(a[0] for side in acts for a in side)), payload, down_weight, *sides[0], *sides[1]
    )
    sides = (values[:6], values[6:])

    hx, hy = swap(hidden, "dp", 1), swap(hidden, "dp", 2)
    down_rows, payload = phase(regroup(down_weight[0], 0, place), payload)
    g1 = swap(payload, "grp", 1)
    last_x, last_y = swap(hy[half:], "dp", 1), swap(hx[:half], "dp", 2)
    blocks = jnp.stack([payload, g1, g2, g3])
    blocks = stack(blocks, to_core(blocks))
    table = blocks[:, rows:, :rows].astype(wide_type).reshape(8, 2, experts, rows)
    scale = lax.dynamic_index_in_dim(table, expert, 2, keepdims=False)
    scale = jnp.sum(scale, axis=1).reshape(8 * rows, 1)
    grads = blocks[:, :rows].reshape(8 * rows, quarter).astype(wide_type)
    grads = (grads * scale).astype(half_type)
    shares = lax.dot_general(down_rows, grads, contract_last, **wide).reshape(4, units, -1)
    sent = shares[3].astype(half_type)
    top, bottom = swap(sent[:half], "dp", 2), swap(sent[half:], "dp", 1)
    sums = [
        stack(shares[1][:half] + top.astype(wide_type), shares[1][half:]).astype(half_type),
        stack(shares[2][:half], shares[2][half:] + bottom.astype(wide_type)).astype(half_type),
    ]
    sums = [swap(value, "dp", j + 1) for j, value in enumerate(sums)]
    own_share, *hidden = phase(shares[0], hidden, hx, hy, last_y, last_x)
    hidden = stack(*hidden)

    out = [
        lax.dot_general(hidden[:, k * 4 * rows : (k + 1) * 4 * rows], down_rows, contract_first, **wide)
        .astype(half_type)
        .astype(wide_type)
        * scale[k * 4 * rows : (k + 1) * 4 * rows]
        for k in range(2)
    ]
    out, hidden, grads = phase(out[0] + to_core(out[1].astype(half_type)).astype(wide_type), hidden, grads)
    back = out[rows:].astype(half_type)
    back = [swap(back[k * rows : (k + 1) * rows], "grp", k + 1) for k in (1, 0, 2)]
    total, *sums = phase(out[:rows], *sums)
    layer_out = total + back[0].astype(wide_type) + back[1].astype(wide_type) + back[2].astype(wide_type)
    down_gradient = jnp.dot(hidden, grads, **wide)
    down_gradient = regroup(down_gradient.astype(half_type), 0, place)

    factors = [beside(*(a[i] for a in side)) for side in acts for i in (1, 2)]
    gate_gradient, up_gradient = in_gradients(
        place.reshape(1).astype(jnp.int32), own_share, sums, factors, sides
    )
    return (layer_out.astype(half_type), gate_gradient[None], up_gradient[None], down_gradient[None])


def body(tokens, grad_out, expert_ids, *rest):
    experts = lax.axis_size(("grp", "loc"))
    rows, per_token = expert_ids.shape
    square = lax.axis_size("dp") == 4 and lax.axis_size("grp") == 4 and lax.axis_size("loc") == 2
    if square and 2 * rows * per_token // experts >= rows:
        return dense_body(tokens, grad_out, expert_ids, *rest)
    return slot_body(tokens, grad_out, expert_ids, *rest)


def solution(mesh):
    return jax.shard_map(
        body,
        mesh=mesh,
        in_specs=(
            P(("grp", "loc"), "dp"),
            P(("grp", "loc"), "dp"),
            P(("grp", "loc"), None),
            P(("grp", "loc"), None),
            P(("grp", "loc"), "dp", None),
            P(("grp", "loc"), "dp", None),
            P(("grp", "loc"), None, "dp"),
        ),
        out_specs=(
            P(("grp", "loc"), "dp"),
            P(("grp", "loc"), "dp", None),
            P(("grp", "loc"), "dp", None),
            P(("grp", "loc"), None, "dp"),
        ),
        check_vma=False,
    )
```

```python
import jax
import jax.numpy as jnp
from jax import lax
from jax.experimental import pallas as pl
from jax.experimental.pallas import tpu as pltpu
from jax.sharding import PartitionSpec as P


def slot_layout(route_ids, experts, capacity):
    flat_ids = route_ids.reshape(-1)
    onehot = (
        flat_ids[:, None] == lax.broadcasted_iota(jnp.int32, (flat_ids.shape[0], experts), 1)
    ).astype(jnp.int32)
    ranks = jnp.sum((jnp.cumsum(onehot, axis=0) - 1) * onehot, axis=1)
    return flat_ids * capacity + ranks


def place_matrix(positions, tok_rows, per_token, slots_total):
    slot_index = lax.broadcasted_iota(jnp.int32, (slots_total, tok_rows, per_token), 0)
    hits = slot_index == positions.reshape(1, tok_rows, per_token)
    return jnp.sum(hits.astype(jnp.float32), axis=2).astype(jnp.bfloat16)


def send_rows(outgoing):
    return lax.all_to_all(outgoing, ("grp", "loc"), split_axis=0, concat_axis=0, tiled=True)


def return_rows(results):
    return lax.all_to_all(results, ("grp", "loc"), split_axis=0, concat_axis=0, tiled=True)


def slot_body(tokens, grad_out, expert_ids, gate_scale, gate_weight, up_weight, down_weight):
    tok_rows, quarter = tokens.shape
    per_token = expert_ids.shape[1]
    experts = lax.axis_size(("grp", "loc"))
    capacity = min(tok_rows, max(2, 2 * tok_rows * per_token // experts))
    slots_total = experts * capacity
    positions = slot_layout(expert_ids, experts, capacity)
    unit_place = place_matrix(positions, tok_rows, per_token, slots_total)
    slot_scale = jnp.zeros((slots_total,), jnp.float32).at[positions].set(gate_scale.reshape(-1))
    picked_grads = jnp.dot(unit_place, grad_out, preferred_element_type=jnp.float32)
    grad_rows = (picked_grads * slot_scale[:, None]).astype(jnp.bfloat16)
    full_tokens = lax.all_gather(tokens, "dp", axis=1, tiled=True)
    features = full_tokens.shape[1]
    token_rows = jnp.dot(unit_place, full_tokens, preferred_element_type=jnp.float32).astype(
        jnp.bfloat16
    )
    outgoing = jnp.concatenate([token_rows, grad_rows], axis=1).reshape(
        experts, capacity, features + quarter
    )
    arrived = send_rows(outgoing)
    slot_tokens = arrived[:, :, :features]
    slot_grads = arrived[:, :, features:]
    flat_tokens = slot_tokens.reshape(slots_total, -1)
    flat_grads = slot_grads.reshape(slots_total, quarter)
    gate_mat = gate_weight[0]
    up_mat = up_weight[0]
    down_mat = down_weight[0]
    feature_contract = (((1,), (1,)), ((), ()))
    gate_pre = lax.dot_general(
        gate_mat, flat_tokens, feature_contract, preferred_element_type=jnp.float32
    )
    up_pre = lax.dot_general(
        up_mat, flat_tokens, feature_contract, preferred_element_type=jnp.float32
    )
    sigmoid_gate = jax.nn.sigmoid(gate_pre)
    activated = gate_pre * sigmoid_gate
    hidden = (activated * up_pre).astype(jnp.bfloat16)
    piece = lax.all_gather(hidden, "dp", axis=0, tiled=True)
    down_rows = down_mat
    out_total = lax.dot_general(
        piece, down_rows, (((0,), (0,)), ((), ())), preferred_element_type=jnp.float32
    )
    block_grad = jnp.dot(piece, flat_grads, preferred_element_type=jnp.float32)
    down_total = block_grad
    out_total, down_total = (out_total, down_total)
    expert_out = out_total.astype(jnp.bfloat16)
    down_gradient = down_total.astype(jnp.bfloat16)
    returned = return_rows(expert_out.reshape(experts, capacity, quarter)).reshape(
        slots_total, quarter
    )
    picked = returned[positions].astype(jnp.float32) * gate_scale.reshape(-1)[:, None]
    layer_out = jnp.sum(picked.reshape(tok_rows, per_token, quarter), axis=1).astype(jnp.bfloat16)
    down_rows = down_mat
    hidden_grad = lax.psum_scatter(
        lax.dot_general(
            down_rows, flat_grads, feature_contract, preferred_element_type=jnp.float32
        ),
        "dp",
        scatter_dimension=0,
        tiled=True,
    )
    gate_grad = (
        hidden_grad * up_pre * sigmoid_gate * (1.0 + gate_pre * (1.0 - sigmoid_gate))
    ).astype(jnp.bfloat16)
    up_grad = (hidden_grad * activated).astype(jnp.bfloat16)
    gate_gradient = jnp.dot(gate_grad, flat_tokens, preferred_element_type=jnp.float32).astype(
        jnp.bfloat16
    )
    up_gradient = jnp.dot(up_grad, flat_tokens, preferred_element_type=jnp.float32).astype(
        jnp.bfloat16
    )
    return (layer_out, gate_gradient[None], up_gradient[None], down_gradient[None])


def swap(value, axis, bit):
    pairs = [(i, i ^ bit) for i in range(lax.axis_size(axis))]
    return lax.ppermute(value, axis, pairs)


def spread(value):
    return [swap(value, "dp", j) for j in (1, 2, 3)]


def to_core(value):
    return swap(value, "loc", 1)


def stack(*values):
    return jnp.concatenate(values, axis=0)


def beside(*values):
    return jnp.concatenate(values, axis=1)


def phase(*values):
    return lax.optimization_barrier(values)


def regroup(value, axis, place):
    size = value.shape[axis] // 4
    return jnp.concatenate(
        [lax.dynamic_slice_in_dim(value, (place ^ j) * size, size, axis) for j in range(4)], axis=axis
    )


def activate(pre):
    units = pre.shape[0] // 2
    gate_pre, up_pre = pre[:units], pre[units:]
    sig = jax.nn.sigmoid(gate_pre)
    activated = gate_pre * sig
    return (activated * up_pre).astype(jnp.bfloat16), up_pre * sig * (1.0 + gate_pre * (1.0 - sig)), activated


def in_gradients(place, own_share, sums, factors, sides):
    units, width = factors[0].shape
    quarter = sides[0][0].shape[1]
    rows = sides[0][0].shape[0] // 4

    def kernel(place_ref, share_ref, x_ref, y_ref, *refs):
        factor_refs, side_refs, (gate_ref, up_ref) = refs[:4], (refs[4:10], refs[10:16]), refs[16:]
        total = share_ref[...] + x_ref[...].astype(jnp.float32) + y_ref[...].astype(jnp.float32)
        lefts = []
        for k in range(2):
            side = total[:, k * width : (k + 1) * width]
            lefts.append([(side * factor_refs[2 * k + i][...]).astype(jnp.bfloat16) for i in range(2)])
        for j in range(4):
            columns = pl.ds(pl.multiple_of((place_ref[0] ^ j) * quarter, quarter), quarter)
            rights = []
            for own_ref, near_ref, *far_refs in side_refs:
                block = pl.ds(j * rows, rows)
                rights.append(jnp.concatenate([own_ref[block], near_ref[block], far_refs[j][...]], axis=0))
            for i, out_ref in enumerate((gate_ref, up_ref)):
                value = jnp.dot(lefts[0][i], rights[0], preferred_element_type=jnp.float32)
                value += jnp.dot(lefts[1][i], rights[1], preferred_element_type=jnp.float32)
                out_ref[:, columns] = value.astype(jnp.bfloat16)

    vmem = pl.BlockSpec(memory_space=pltpu.VMEM)
    return pl.pallas_call(
        kernel,
        out_shape=[jax.ShapeDtypeStruct((units, 4 * quarter), jnp.bfloat16)] * 2,
        in_specs=[pl.BlockSpec(memory_space=pltpu.SMEM)] + [vmem] * 19,
        out_specs=[vmem] * 2,
        compiler_params=pltpu.CompilerParams(vmem_limit_bytes=20 * 2**20),
    )(place, own_share, *sums, *factors, *sides[0], *sides[1])


def dense_body(tokens, grad_out, expert_ids, gate_scale, gate_weight, up_weight, down_weight):
    rows, quarter = tokens.shape
    experts = lax.axis_size(("grp", "loc"))
    place = lax.axis_index("dp")
    expert = lax.axis_index(("grp", "loc"))
    units = gate_weight.shape[1]
    half = units // 2
    contract_last = (((1,), (1,)), ((), ()))
    contract_first = (((0,), (0,)), ((), ()))
    wide = dict(preferred_element_type=jnp.float32)
    half_type, wide_type = jnp.bfloat16, jnp.float32

    def dot_part(weights, j, part):
        weights = lax.dynamic_slice_in_dim(weights, (place ^ j) * quarter, quarter, 1)
        return lax.dot_general(weights, part, contract_last, **wide)

    def block_part(weights, block):
        return sum(dot_part(weights, j, block[j * rows : (j + 1) * rows]) for j in range(4))

    t2, t3 = swap(tokens, "grp", 2), swap(tokens, "grp", 3)
    p0 = [tokens] + spread(tokens)
    in_weights = stack(gate_weight[0], up_weight[0])
    named = lax.broadcasted_iota(jnp.int32, (experts, rows, 1), 0) == expert_ids[None]
    scales = jnp.sum(jnp.where(named, gate_scale[None], 0.0), axis=2)
    high = lax.reduce_precision(scales, 8, 7)
    table = stack(high, scales - high).astype(half_type)
    table = jnp.pad(table, ((0, 0), (0, quarter - rows)))
    payload = stack(grad_out, table)
    own = stack(*p0)
    p1 = swap(own, "grp", 1)
    own, far, payload, in_weights, *p0 = phase(own, stack(t2, t3), payload, in_weights, *p0)
    own_there, far_there = to_core(own), to_core(far)
    pre_own = [block_part(in_weights, block) for block in (own, own_there)]
    pre_far = [dot_part(in_weights, 0, block) for block in (far, far_there)]

    p2 = [far] + spread(far)
    late, own_there = phase(payload, own_there)
    g2 = swap(late, "grp", 2)
    late, p1, *pre_own = phase(payload, p1, *pre_own)
    g3 = swap(late, "grp", 3)
    p1_there = to_core(p1)
    pre_near = [block_part(in_weights, block) for block in (p1, p1_there)]
    values = phase(*p2, payload, p1, p1_there, far_there, *pre_far, *pre_own, *pre_near)
    p2, (payload, p1, p1_there, far_there), pre_far = values[:4], values[4:8], list(values[8:10])
    pre_own, pre_near = values[10:12], values[12:]

    p2_there = [far_there] + [to_core(block) for block in p2[1:]]
    acts = []
    for k, (near, far_parts) in enumerate(((p1, p2), (p1_there, p2_there))):
        for j in (1, 2, 3):
            pre_far[k] = pre_far[k] + dot_part(in_weights, j, far_parts[j])
        acts.append([activate(pre) for pre in (pre_own[k], pre_near[k], pre_far[k])])
    sides = ((own, p1, *p2), (own_there, p1_there, *p2_there))
    hidden, payload, down_weight, *values = phase(
        beside(*(a[0] for side in acts for a in side)), payload, down_weight, *sides[0], *sides[1]
    )
    sides = (values[:6], values[6:])

    hx, hy = swap(hidden, "dp", 1), swap(hidden, "dp", 2)
    down_rows, payload = phase(regroup(down_weight[0], 0, place), payload)
    g1 = swap(payload, "grp", 1)
    last_x, last_y = swap(hy[half:], "dp", 1), swap(hx[:half], "dp", 2)
    blocks = jnp.stack([payload, g1, g2, g3])
    blocks = stack(blocks, to_core(blocks))
    table = blocks[:, rows:, :rows].astype(wide_type).reshape(8, 2, experts, rows)
    scale = lax.dynamic_index_in_dim(table, expert, 2, keepdims=False)
    scale = jnp.sum(scale, axis=1).reshape(8 * rows, 1)
    grads = blocks[:, :rows].reshape(8 * rows, quarter).astype(wide_type)
    grads = (grads * scale).astype(half_type)
    shares = lax.dot_general(down_rows, grads, contract_last, **wide).reshape(4, units, -1)
    sent = shares[3].astype(half_type)
    top, bottom = swap(sent[:half], "dp", 2), swap(sent[half:], "dp", 1)
    sums = [
        stack(shares[1][:half] + top.astype(wide_type), shares[1][half:]).astype(half_type),
        stack(shares[2][:half], shares[2][half:] + bottom.astype(wide_type)).astype(half_type),
    ]
    sums = [swap(value, "dp", j + 1) for j, value in enumerate(sums)]
    own_share, *hidden = phase(shares[0], hidden, hx, hy, last_y, last_x)
    hidden = stack(*hidden)

    out = [
        lax.dot_general(hidden[:, k * 4 * rows : (k + 1) * 4 * rows], down_rows, contract_first, **wide)
        .astype(half_type)
        .astype(wide_type)
        * scale[k * 4 * rows : (k + 1) * 4 * rows]
        for k in range(2)
    ]
    theirs = to_core(out[1].astype(half_type))
    out_own, own_share = phase(out[0], own_share)
    out, hidden, grads = phase(out_own + theirs.astype(wide_type), hidden, grads)
    back = out[rows:].astype(half_type)
    back = [swap(back[k * rows : (k + 1) * rows], "grp", k + 1) for k in (1, 0, 2)]
    total, *sums = phase(out[:rows], *sums)
    layer_out = total + back[0].astype(wide_type) + back[1].astype(wide_type) + back[2].astype(wide_type)
    down_gradient = jnp.dot(hidden, grads, **wide)
    down_gradient = regroup(down_gradient.astype(half_type), 0, place)

    factors = [beside(*(a[i] for a in side)) for side in acts for i in (1, 2)]
    gate_gradient, up_gradient = in_gradients(
        place.reshape(1).astype(jnp.int32), own_share, sums, factors, sides
    )
    return (layer_out.astype(half_type), gate_gradient[None], up_gradient[None], down_gradient[None])


def body(tokens, grad_out, expert_ids, *rest):
    experts = lax.axis_size(("grp", "loc"))
    rows, per_token = expert_ids.shape
    square = lax.axis_size("dp") == 4 and lax.axis_size("grp") == 4 and lax.axis_size("loc") == 2
    if square and 2 * rows * per_token // experts >= rows:
        return dense_body(tokens, grad_out, expert_ids, *rest)
    return slot_body(tokens, grad_out, expert_ids, *rest)


def solution(mesh):
    return jax.shard_map(
        body,
        mesh=mesh,
        in_specs=(
            P(("grp", "loc"), "dp"),
            P(("grp", "loc"), "dp"),
            P(("grp", "loc"), None),
            P(("grp", "loc"), None),
            P(("grp", "loc"), "dp", None),
            P(("grp", "loc"), "dp", None),
            P(("grp", "loc"), None, "dp"),
        ),
        out_specs=(
            P(("grp", "loc"), "dp"),
            P(("grp", "loc"), "dp", None),
            P(("grp", "loc"), "dp", None),
            P(("grp", "loc"), None, "dp"),
        ),
        check_vma=False,
    )
```

```python
import jax
import jax.numpy as jnp
from jax import lax
from jax.experimental import pallas as pl
from jax.experimental.pallas import tpu as pltpu
from jax.sharding import PartitionSpec as P


def slot_layout(route_ids, experts, capacity):
    flat_ids = route_ids.reshape(-1)
    onehot = (
        flat_ids[:, None] == lax.broadcasted_iota(jnp.int32, (flat_ids.shape[0], experts), 1)
    ).astype(jnp.int32)
    ranks = jnp.sum((jnp.cumsum(onehot, axis=0) - 1) * onehot, axis=1)
    return flat_ids * capacity + ranks


def place_matrix(positions, tok_rows, per_token, slots_total):
    slot_index = lax.broadcasted_iota(jnp.int32, (slots_total, tok_rows, per_token), 0)
    hits = slot_index == positions.reshape(1, tok_rows, per_token)
    return jnp.sum(hits.astype(jnp.float32), axis=2).astype(jnp.bfloat16)


def send_rows(outgoing):
    return lax.all_to_all(outgoing, ("grp", "loc"), split_axis=0, concat_axis=0, tiled=True)


def return_rows(results):
    return lax.all_to_all(results, ("grp", "loc"), split_axis=0, concat_axis=0, tiled=True)


def slot_body(tokens, grad_out, expert_ids, gate_scale, gate_weight, up_weight, down_weight):
    tok_rows, quarter = tokens.shape
    per_token = expert_ids.shape[1]
    experts = lax.axis_size(("grp", "loc"))
    capacity = min(tok_rows, max(2, 2 * tok_rows * per_token // experts))
    slots_total = experts * capacity
    positions = slot_layout(expert_ids, experts, capacity)
    unit_place = place_matrix(positions, tok_rows, per_token, slots_total)
    slot_scale = jnp.zeros((slots_total,), jnp.float32).at[positions].set(gate_scale.reshape(-1))
    picked_grads = jnp.dot(unit_place, grad_out, preferred_element_type=jnp.float32)
    grad_rows = (picked_grads * slot_scale[:, None]).astype(jnp.bfloat16)
    full_tokens = lax.all_gather(tokens, "dp", axis=1, tiled=True)
    features = full_tokens.shape[1]
    token_rows = jnp.dot(unit_place, full_tokens, preferred_element_type=jnp.float32).astype(
        jnp.bfloat16
    )
    outgoing = jnp.concatenate([token_rows, grad_rows], axis=1).reshape(
        experts, capacity, features + quarter
    )
    arrived = send_rows(outgoing)
    slot_tokens = arrived[:, :, :features]
    slot_grads = arrived[:, :, features:]
    flat_tokens = slot_tokens.reshape(slots_total, -1)
    flat_grads = slot_grads.reshape(slots_total, quarter)
    gate_mat = gate_weight[0]
    up_mat = up_weight[0]
    down_mat = down_weight[0]
    feature_contract = (((1,), (1,)), ((), ()))
    gate_pre = lax.dot_general(
        gate_mat, flat_tokens, feature_contract, preferred_element_type=jnp.float32
    )
    up_pre = lax.dot_general(
        up_mat, flat_tokens, feature_contract, preferred_element_type=jnp.float32
    )
    sigmoid_gate = jax.nn.sigmoid(gate_pre)
    activated = gate_pre * sigmoid_gate
    hidden = (activated * up_pre).astype(jnp.bfloat16)
    piece = lax.all_gather(hidden, "dp", axis=0, tiled=True)
    down_rows = down_mat
    out_total = lax.dot_general(
        piece, down_rows, (((0,), (0,)), ((), ())), preferred_element_type=jnp.float32
    )
    block_grad = jnp.dot(piece, flat_grads, preferred_element_type=jnp.float32)
    down_total = block_grad
    out_total, down_total = (out_total, down_total)
    expert_out = out_total.astype(jnp.bfloat16)
    down_gradient = down_total.astype(jnp.bfloat16)
    returned = return_rows(expert_out.reshape(experts, capacity, quarter)).reshape(
        slots_total, quarter
    )
    picked = returned[positions].astype(jnp.float32) * gate_scale.reshape(-1)[:, None]
    layer_out = jnp.sum(picked.reshape(tok_rows, per_token, quarter), axis=1).astype(jnp.bfloat16)
    down_rows = down_mat
    hidden_grad = lax.psum_scatter(
        lax.dot_general(
            down_rows, flat_grads, feature_contract, preferred_element_type=jnp.float32
        ),
        "dp",
        scatter_dimension=0,
        tiled=True,
    )
    gate_grad = (
        hidden_grad * up_pre * sigmoid_gate * (1.0 + gate_pre * (1.0 - sigmoid_gate))
    ).astype(jnp.bfloat16)
    up_grad = (hidden_grad * activated).astype(jnp.bfloat16)
    gate_gradient = jnp.dot(gate_grad, flat_tokens, preferred_element_type=jnp.float32).astype(
        jnp.bfloat16
    )
    up_gradient = jnp.dot(up_grad, flat_tokens, preferred_element_type=jnp.float32).astype(
        jnp.bfloat16
    )
    return (layer_out, gate_gradient[None], up_gradient[None], down_gradient[None])


def swap(value, axis, bit):
    pairs = [(i, i ^ bit) for i in range(lax.axis_size(axis))]
    return lax.ppermute(value, axis, pairs)


def spread(value):
    return [swap(value, "dp", j) for j in (1, 2, 3)]


def to_core(value):
    return swap(value, "loc", 1)


def stack(*values):
    return jnp.concatenate(values, axis=0)


def beside(*values):
    return jnp.concatenate(values, axis=1)


def phase(*values):
    return lax.optimization_barrier(values)


def regroup(value, axis, place):
    size = value.shape[axis] // 4
    return jnp.concatenate(
        [lax.dynamic_slice_in_dim(value, (place ^ j) * size, size, axis) for j in range(4)], axis=axis
    )


def activate(pre):
    units = pre.shape[0] // 2
    gate_pre, up_pre = pre[:units], pre[units:]
    sig = jax.nn.sigmoid(gate_pre)
    activated = gate_pre * sig
    return (activated * up_pre).astype(jnp.bfloat16), up_pre * sig * (1.0 + gate_pre * (1.0 - sig)), activated


def in_gradients(place, own_share, sums, factors, sides):
    units, width = factors[0].shape
    quarter = sides[0][0].shape[1]
    rows = sides[0][0].shape[0] // 4

    def kernel(place_ref, share_ref, x_ref, y_ref, *refs):
        factor_refs, side_refs, (gate_ref, up_ref) = refs[:4], (refs[4:10], refs[10:16]), refs[16:]
        total = share_ref[...] + x_ref[...].astype(jnp.float32) + y_ref[...].astype(jnp.float32)
        lefts = []
        for k in range(2):
            side = total[:, k * width : (k + 1) * width]
            lefts.append([(side * factor_refs[2 * k + i][...]).astype(jnp.bfloat16) for i in range(2)])
        for j in range(4):
            columns = pl.ds(pl.multiple_of((place_ref[0] ^ j) * quarter, quarter), quarter)
            rights = []
            for own_ref, near_ref, *far_refs in side_refs:
                block = pl.ds(j * rows, rows)
                rights.append(jnp.concatenate([own_ref[block], near_ref[block], far_refs[j][...]], axis=0))
            for i, out_ref in enumerate((gate_ref, up_ref)):
                value = jnp.dot(lefts[0][i], rights[0], preferred_element_type=jnp.float32)
                value += jnp.dot(lefts[1][i], rights[1], preferred_element_type=jnp.float32)
                out_ref[:, columns] = value.astype(jnp.bfloat16)

    vmem = pl.BlockSpec(memory_space=pltpu.VMEM)
    return pl.pallas_call(
        kernel,
        out_shape=[jax.ShapeDtypeStruct((units, 4 * quarter), jnp.bfloat16)] * 2,
        in_specs=[pl.BlockSpec(memory_space=pltpu.SMEM)] + [vmem] * 19,
        out_specs=[vmem] * 2,
        compiler_params=pltpu.CompilerParams(vmem_limit_bytes=20 * 2**20),
    )(place, own_share, *sums, *factors, *sides[0], *sides[1])


def dense_body(tokens, grad_out, expert_ids, gate_scale, gate_weight, up_weight, down_weight):
    rows, quarter = tokens.shape
    experts = lax.axis_size(("grp", "loc"))
    place = lax.axis_index("dp")
    expert = lax.axis_index(("grp", "loc"))
    units = gate_weight.shape[1]
    half = units // 2
    contract_last = (((1,), (1,)), ((), ()))
    contract_first = (((0,), (0,)), ((), ()))
    wide = dict(preferred_element_type=jnp.float32)
    half_type, wide_type = jnp.bfloat16, jnp.float32

    def dot_part(weights, j, part):
        weights = lax.dynamic_slice_in_dim(weights, (place ^ j) * quarter, quarter, 1)
        return lax.dot_general(weights, part, contract_last, **wide)

    def block_part(weights, block):
        return sum(dot_part(weights, j, block[j * rows : (j + 1) * rows]) for j in range(4))

    t2, t3 = swap(tokens, "grp", 2), swap(tokens, "grp", 3)
    p0 = [tokens] + spread(tokens)
    in_weights = stack(gate_weight[0], up_weight[0])
    named = lax.broadcasted_iota(jnp.int32, (experts, rows, 1), 0) == expert_ids[None]
    scales = jnp.sum(jnp.where(named, gate_scale[None], 0.0), axis=2)
    high = lax.reduce_precision(scales, 8, 7)
    table = stack(high, scales - high).astype(half_type)
    table = jnp.pad(table, ((0, 0), (0, quarter - rows)))
    payload = stack(grad_out, table)
    own = stack(*p0)
    p1 = swap(own, "grp", 1)
    own, far, payload, in_weights, *p0 = phase(own, stack(t2, t3), payload, in_weights, *p0)
    own_there, far_there = to_core(own), to_core(far)
    pre_own = [block_part(in_weights, block) for block in (own, own_there)]
    pre_far = [dot_part(in_weights, 0, block) for block in (far, far_there)]

    p2 = [far] + spread(far)
    late, own_there = phase(payload, own_there)
    g2 = swap(late, "grp", 2)
    late, p1, *pre_own, pre_far[0], pre_far[1] = phase(payload, p1, *pre_own, *pre_far)
    g3 = swap(late, "grp", 3)
    p1_there = to_core(p1)
    pre_near = [block_part(in_weights, block) for block in (p1, p1_there)]
    values = phase(*p2, payload, p1, p1_there, far_there, *pre_far, *pre_own, *pre_near)
    p2, (payload, p1, p1_there, far_there), pre_far = values[:4], values[4:8], list(values[8:10])
    pre_own, pre_near = values[10:12], values[12:]

    p2_there = [far_there] + [to_core(block) for block in p2[1:]]
    acts = []
    for k, (near, far_parts) in enumerate(((p1, p2), (p1_there, p2_there))):
        for j in (1, 2, 3):
            pre_far[k] = pre_far[k] + dot_part(in_weights, j, far_parts[j])
        acts.append([activate(pre) for pre in (pre_own[k], pre_near[k], pre_far[k])])
    sides = ((own, p1, *p2), (own_there, p1_there, *p2_there))
    hidden, payload, down_weight, *values = phase(
        beside(*(a[0] for side in acts for a in side)), payload, down_weight, *sides[0], *sides[1]
    )
    sides = (values[:6], values[6:])

    hx, hy = swap(hidden, "dp", 1), swap(hidden, "dp", 2)
    down_rows, payload = phase(regroup(down_weight[0], 0, place), payload)
    g1 = swap(payload, "grp", 1)
    last_x, last_y = swap(hy[half:], "dp", 1), swap(hx[:half], "dp", 2)
    blocks = jnp.stack([payload, g1, g2, g3])
    blocks = stack(blocks, to_core(blocks))
    table = blocks[:, rows:, :rows].astype(wide_type).reshape(8, 2, experts, rows)
    scale = lax.dynamic_index_in_dim(table, expert, 2, keepdims=False)
    scale = jnp.sum(scale, axis=1).reshape(8 * rows, 1)
    grads = blocks[:, :rows].reshape(8 * rows, quarter).astype(wide_type)
    grads = (grads * scale).astype(half_type)
    shares = lax.dot_general(down_rows, grads, contract_last, **wide).reshape(4, units, -1)
    sent = shares[3].astype(half_type)
    top, bottom = swap(sent[:half], "dp", 2), swap(sent[half:], "dp", 1)
    sums = [
        stack(shares[1][:half] + top.astype(wide_type), shares[1][half:]).astype(half_type),
        stack(shares[2][:half], shares[2][half:] + bottom.astype(wide_type)).astype(half_type),
    ]
    sums = [swap(value, "dp", j + 1) for j, value in enumerate(sums)]
    own_share, *hidden = phase(shares[0], hidden, hx, hy, last_y, last_x)
    hidden = stack(*hidden)

    out = [
        lax.dot_general(hidden[:, k * 4 * rows : (k + 1) * 4 * rows], down_rows, contract_first, **wide)
        .astype(half_type)
        .astype(wide_type)
        * scale[k * 4 * rows : (k + 1) * 4 * rows]
        for k in range(2)
    ]
    theirs = to_core(out[1].astype(half_type))
    out_own, own_share = phase(out[0], own_share)
    out, hidden, grads = phase(out_own + theirs.astype(wide_type), hidden, grads)
    back = out[rows:].astype(half_type)
    back = [swap(back[k * rows : (k + 1) * rows], "grp", k + 1) for k in (1, 0, 2)]
    total, *sums = phase(out[:rows], *sums)
    layer_out = total + back[0].astype(wide_type) + back[1].astype(wide_type) + back[2].astype(wide_type)
    down_gradient = jnp.dot(hidden, grads, **wide)
    down_gradient = regroup(down_gradient.astype(half_type), 0, place)

    factors = [beside(*(a[i] for a in side)) for side in acts for i in (1, 2)]
    gate_gradient, up_gradient = in_gradients(
        place.reshape(1).astype(jnp.int32), own_share, sums, factors, sides
    )
    return (layer_out.astype(half_type), gate_gradient[None], up_gradient[None], down_gradient[None])


def body(tokens, grad_out, expert_ids, *rest):
    experts = lax.axis_size(("grp", "loc"))
    rows, per_token = expert_ids.shape
    square = lax.axis_size("dp") == 4 and lax.axis_size("grp") == 4 and lax.axis_size("loc") == 2
    if square and 2 * rows * per_token // experts >= rows:
        return dense_body(tokens, grad_out, expert_ids, *rest)
    return slot_body(tokens, grad_out, expert_ids, *rest)


def solution(mesh):
    return jax.shard_map(
        body,
        mesh=mesh,
        in_specs=(
            P(("grp", "loc"), "dp"),
            P(("grp", "loc"), "dp"),
            P(("grp", "loc"), None),
            P(("grp", "loc"), None),
            P(("grp", "loc"), "dp", None),
            P(("grp", "loc"), "dp", None),
            P(("grp", "loc"), None, "dp"),
        ),
        out_specs=(
            P(("grp", "loc"), "dp"),
            P(("grp", "loc"), "dp", None),
            P(("grp", "loc"), "dp", None),
            P(("grp", "loc"), None, "dp"),
        ),
        check_vma=False,
    )
```
